256 devices in a mesh: gz: 4 (over y), grid: 64 (over z, x, core).
Axes of the slice: x: 4, y: 4, z: 8, core: 2. Of those that a mesh axis runs over, the one named last changes fastest.
Arguments:
- leaf_rhs: bfloat16 [4, 1024, 128, 256], P('gz', 'grid'), may hold values from -6 to 6
- leaf_inverse: bfloat16 [4, 1024, 128, 128], P('gz', 'grid'), may hold values from -0.5 to 0.5
- leaf_update: bfloat16 [4, 1024, 128, 128], P('gz', 'grid'), may hold values from -0.125 to 0.125
- leaf_target: int32 [4, 1024, 1], P('gz', 'grid'), may hold values from 0 to 63; in each aligned block of 16 rows (0 to 15, 16 to 31, ..., all dimensions but the last counted through in order) at most 2 rows name the same one
- anc_rhs: float32 [64, 128, 256], P('grid'), may hold values from -6 to 6
- anc_inverse: float32 [64, 128, 128], P('grid'), may hold values from -0.4 to 1.8, as said below
- anc_coupling: float32 [64, 128, 128], P('grid'), may hold values from -256 to 256, as said below
Outputs:
- leaf_solution: bfloat16 [4, 1024, 128, 256], P('gz', 'grid')
- anc_solution: float32 [64, 128, 256], P('grid')
The draws below stay inside these ranges and needn't reach their ends.
Inputs may be any that keep to these rules, and one draw needn't show every extreme that they name: `leaf_target`: among the 16 leaves of one device at most 2 update the same ancestor. `anc_inverse`: dense blocks. `anc_coupling`: dense blocks.
All inputs are finite; a program needn't handle non-finite values.
Results may differ from the reference program's by a relative error of at most 0.0085.
Values may be sent and summed in bfloat16 or wider, within the bound.
No kernel may reach another device: no remote copies, remote signals or barrier semaphores. Data moves between devices by JAX's collectives and lax.ppermute only.
A program may use at most 128 MiB of HBM per device.

```python
import math
import jax
import jax.numpy as jnp
import numpy as np
from jax import lax

W = 128
R = 256
LEAF_DEV = 16
LAYERS = 4
ANCESTOR_CHAIN = 64
LEAVES = 1024
CAP = 2


def chain_law(key):
    baseline_value = jax.random.fold_in(key, 7)
    share_slow = 0.5
    slow_flag = jax.random.bernoulli(jax.random.fold_in(baseline_value, 1), share_slow, (W,))
    fast_keep = jax.random.uniform(jax.random.fold_in(baseline_value, 2), (W,), jnp.float32, 0.3, 0.7)
    baseline_loss = jnp.where(slow_flag, jnp.log(2.0) / ANCESTOR_CHAIN, -jnp.log(fast_keep))
    spread_amount = jnp.exp(jax.random.uniform(jax.random.fold_in(baseline_value, 3), (ANCESTOR_CHAIN, W), jnp.float32, jnp.log(0.7), jnp.log(1.4)))
    spike_positions = jax.random.randint(jax.random.fold_in(baseline_value, 4), (3,), 0, ANCESTOR_CHAIN)
    spike_flag = jnp.any(jnp.arange(ANCESTOR_CHAIN)[:, None] == spike_positions[None, :], axis=1)
    loss_value = baseline_loss[None, :] * spread_amount + jnp.where(spike_flag, jnp.log(4.0 / 3.0), 0.0)[:, None]
    keep_rate = jnp.exp(-loss_value)
    level = (1.0 - jnp.exp(-baseline_loss)) * jnp.exp(jax.random.uniform(jax.random.fold_in(baseline_value, 5), (W,), jnp.float32, jnp.log(0.5), jnp.log(2.0)))
    return (keep_rate, level)


def mixing(key, salt):
    shape = (ANCESTOR_CHAIN, W, W)
    noise_key = jax.random.fold_in(key, salt)
    noise = jnp.clip(0.2 * jax.random.normal(noise_key, shape, jnp.float32), -1.0, 1.0)
    return noise / jnp.sqrt(W * 1.0) + jnp.eye(W, dtype=jnp.float32)[None, :, :]


def draw_anc_inverse(key, part):
    keep_rate, level = chain_law(key)
    return level[None, :, None] * mixing(key, 11)


def draw_anc_coupling(key, part):
    keep_rate, level = chain_law(key)
    return -mixing(key, 12) * (keep_rate / level[None, :])[:, None, :]


def shard_levels(key, dims, cuts, low, high):
    level = 1.0
    for position, shards_of in cuts:
        heights = jax.random.uniform(jax.random.fold_in(jax.random.fold_in(key, 6), position), (shards_of,), jnp.float32, low / len(cuts), high / len(cuts))
        level = level * jnp.repeat(jnp.exp(heights), dims[position] // shards_of).reshape((-1,) + (1,) * (len(dims) - 1 - position))
    return level


def routed_block(stream_key, own, number, rows, amount, top, most, slope):
    ranking = jax.random.permutation(stream_key, amount)
    crowded, common = shares(amount, rows * top, most, slope, True), shares(amount, rows * top, most, slope, False)
    places = jnp.arange(amount)

    def named(tallies, turn):
        used = int((tallies > 0).sum())
        fixed = max(1, used // 4)
        shifted = fixed + (places - fixed + turn * (used - fixed)) % max(1, amount - fixed)
        return jnp.zeros((amount,), jnp.int32).at[ranking[jnp.where(places < fixed, places, shifted)]].set(jnp.asarray(tallies, jnp.int32))

    tallies = jnp.where(number % 4 == 0, named(crowded, number // 4), named(common, number - number // 4 - 1))
    mixed = jax.random.permutation(jax.random.fold_in(own, 3), amount)
    giver, taker = mixed[0:amount // 2 * 2:2], mixed[1:amount // 2 * 2:2]
    room = jnp.minimum(tallies[giver] - 1, most - tallies[taker]) // 2
    room = jnp.where((giver == ranking[0]) | (taker == ranking[0]) | (tallies[taker] == 0), 0, jnp.maximum(room, 0))
    shifted = jax.random.randint(jax.random.fold_in(own, 4), (amount // 2,), 0, 1 << 20) % (room + 1)
    tallies = tallies.at[giver].add(-shifted).at[taker].add(shifted)
    labels = jnp.searchsorted(jnp.cumsum(tallies), jnp.arange(rows * top), side="right").astype(jnp.int32)
    table = labels.reshape(top, rows).T
    table = table[jax.random.permutation(jax.random.fold_in(own, 1), rows)]
    turn = jax.random.randint(jax.random.fold_in(own, 2), (rows, 1), 0, top)
    return jnp.take_along_axis(table, (jnp.arange(top)[None, :] + turn) % top, axis=1)


def shares(amount, total, reach, skew, full):
    portions = [(1 << 20) // math.isqrt(standing ** skew) + 1 for standing in range(1, amount + 1)]
    largest = reach if full else min(reach, max(-(-total // amount), total * portions[0] // sum(portions)))
    least = 1 if total - largest >= amount - 1 else 0
    holding, surplus = [largest] + [least] * (amount - 1), total - largest - least * (amount - 1)
    while surplus > 0:
        candidates = [i for i in range(1, amount) if holding[i] < largest] or [i for i in range(1, amount) if holding[i] < reach]
        mass, remaining = sum([portions[i] for i in candidates]), surplus
        for i in candidates:
            addition = min(reach - holding[i], max(1, remaining * portions[i] // mass), surplus)
            holding[i] = holding[i] + addition
            surplus = surplus - addition
    return np.array(holding)


def normal_values(stream_key, shape, width, reach, shards=(), kind=jnp.bfloat16):
    values = width * jax.random.normal(stream_key, shape, jnp.float32)
    if shards:
        values = values * shard_levels(stream_key, shape, shards, -0.22, 0.18)
    return jnp.clip(values, -reach, reach).astype(kind)


def setup_inputs(seed: int = 0) -> dict:
    key_list = jax.random.split(jax.random.key(seed), 8)
    leaf_rhs = normal_values(key_list[0], (LAYERS, LEAVES, W, R), 1.0, 6.0, ((0, 4), (1, 64)))
    leaf_inverse = normal_values(key_list[1], (LAYERS, LEAVES, W, W), W ** -0.5, 0.5, ((0, 4), (1, 64)))
    leaf_update = normal_values(key_list[2], (LAYERS, LEAVES, W, W), (W * LAYERS * LEAF_DEV // 4) ** -0.5, 0.125, ((0, 4), (1, 64)))
    leaf_target_keys = jax.random.split(jax.random.fold_in(key_list[3], 1), LAYERS * LEAVES // LEAF_DEV)
    leaf_target_turns = jax.random.permutation(jax.random.fold_in(key_list[3], 3), LAYERS * LEAVES // LEAF_DEV)
    leaf_target = jax.vmap(lambda own, number: routed_block(jax.random.fold_in(key_list[3], 2), own, number, LEAF_DEV, ANCESTOR_CHAIN, 1, CAP, 2))(leaf_target_keys, leaf_target_turns).reshape((LAYERS, LEAVES, 1))
    anc_rhs = normal_values(key_list[4], (ANCESTOR_CHAIN, W, R), 1.0, 6.0, ((0, 64),), jnp.float32)
    anc_inverse = draw_anc_inverse(jax.random.fold_in(key_list[7], 71), 0)
    anc_coupling = draw_anc_coupling(jax.random.fold_in(key_list[7], 71), 0)
    return {"leaf_rhs": leaf_rhs, "leaf_inverse": leaf_inverse, "leaf_update": leaf_update, "leaf_target": leaf_target, "anc_rhs": anc_rhs, "anc_inverse": anc_inverse, "anc_coupling": anc_coupling}


def widen(value):
    return lax.optimization_barrier(value).astype(jnp.float32)


def reference(leaf_rhs, leaf_inverse, leaf_update, leaf_target, anc_rhs, anc_inverse, anc_coupling):
    precise = lax.Precision.HIGHEST
    groups = LAYERS * ANCESTOR_CHAIN
    grouped_rhs = leaf_rhs.reshape(groups, LEAF_DEV, W, R)
    grouped_inverse = leaf_inverse.reshape(groups, LEAF_DEV, W, W)
    grouped_update = leaf_update.reshape(groups, LEAF_DEV, W, W)
    grouped_target = leaf_target.reshape(groups, LEAF_DEV).astype(jnp.int32)
    owners = jnp.arange(ANCESTOR_CHAIN, dtype=jnp.int32)

    def forward_step(running, blocks):
        inverse_block, rhs_block, update_block, target_block = blocks
        forward = jnp.einsum("kij,kjr->kir", inverse_block.astype(jnp.float32), rhs_block.astype(jnp.float32), precision=precise).astype(jnp.bfloat16)
        update = jnp.einsum("kij,kjr->kir", update_block.astype(jnp.float32), widen(forward), precision=precise).astype(jnp.bfloat16)
        onehot = (owners[:, None] == target_block[None, :]).astype(jnp.float32)
        partial_sum = jnp.einsum("tk,kir->tir", onehot, widen(update), precision=precise).astype(jnp.bfloat16)
        running = running + widen(partial_sum)
        return running, forward

    totals, forwards = lax.scan(forward_step, jnp.zeros((ANCESTOR_CHAIN, W, R), jnp.float32), (grouped_inverse, grouped_rhs, grouped_update, grouped_target))
    reduced = anc_rhs - totals

    def chain_forward(previous, blocks):
        inverse_block, coupling_block, reduced_block = blocks
        current = jnp.dot(inverse_block, reduced_block - jnp.dot(coupling_block, previous, precision=precise), precision=precise)
        return current, current

    zero_block = jnp.zeros((W, R), jnp.float32)
    final_forward, solved = lax.scan(chain_forward, zero_block, (anc_inverse, anc_coupling, reduced))
    next_coupling = jnp.concatenate([anc_coupling[1:], jnp.zeros((1, W, W), jnp.float32)], axis=0)

    def chain_backward(following, blocks):
        inverse_block, coupling_block, solved_block = blocks
        current = jnp.dot(inverse_block.T, solved_block - jnp.dot(coupling_block.T, following, precision=precise), precision=precise)
        return current, current

    final_backward, anc_solution = lax.scan(chain_backward, zero_block, (anc_inverse, next_coupling, solved), reverse=True)
    rounded = widen(anc_solution.astype(jnp.bfloat16))

    def backward_step(carry_value, blocks):
        inverse_block, update_block, target_block, forward = blocks
        onehot = (target_block[:, None] == owners[None, :]).astype(jnp.float32)
        chosen = jnp.einsum("kt,tir->kir", onehot, rounded, precision=precise)
        correction = jnp.einsum("kji,kjr->kir", update_block.astype(jnp.float32), chosen, precision=precise)
        residue = (widen(forward) - correction).astype(jnp.bfloat16)
        result = jnp.einsum("kji,kjr->kir", inverse_block.astype(jnp.float32), widen(residue), precision=precise).astype(jnp.bfloat16)
        return carry_value, result

    final_carry, results = lax.scan(backward_step, jnp.zeros((), jnp.float32), (grouped_inverse, grouped_update, grouped_target, forwards))
    leaf_solution = results.reshape(LAYERS, ANCESTOR_CHAIN * LEAF_DEV, W, R)
    return (leaf_solution, anc_solution)
```

```python
import functools

import jax
import jax.numpy as jnp
from jax import lax
from jax.experimental import pallas as pl
from jax.experimental.pallas import tpu as pltpu
from jax.sharding import Mesh
from jax.sharding import PartitionSpec as P

F32 = jnp.float32
BF16 = jnp.bfloat16
PLANE_AXES = ("y", "x", "c")
STEP_SCALE = 2.0**-8
CHAIN_BLOCK = 4


def dot_nn(a, b):
    return lax.dot_general(
        a, b, (((1,), (0,)), ((), ())), precision=lax.Precision.HIGHEST, preferred_element_type=F32
    )


def dot_nt(a, b):
    return lax.dot_general(
        a, b, (((1,), (1,)), ((), ())), precision=lax.Precision.HIGHEST, preferred_element_type=F32
    )


def leaf_forward_kernel(peers, y_ref, rhs_ref, inv_ref, upd_ref, tgt_ref, anc_ref, fwd_ref, send_ref):
    step = pl.program_id(0)
    last = pl.num_programs(0) - 1
    rhs_count, width = fwd_ref.shape[1:]
    cols = rhs_count // peers

    @pl.when(step < last)
    def _():
        parts = []
        for k in range(2):
            forward = lax.dot_general(
                rhs_ref[k], inv_ref[k], (((0,), (1,)), ((), ())), preferred_element_type=F32
            ).astype(BF16)
            fwd_ref[k] = forward
            update = lax.dot_general(
                forward, upd_ref[k], (((1,), (1,)), ((), ())), preferred_element_type=F32
            )
            parts.append(update.reshape(peers, cols, width))
        send_ref[...] = jnp.concatenate(parts, axis=1).astype(BF16)

    @pl.when(step == last)
    def _():
        rows = anc_ref[...].T
        high = rows.astype(BF16).astype(F32)
        low = rows - high
        layer = y_ref[0]
        mine = jnp.where(layer == 0, high, jnp.where(layer == 1, low, jnp.zeros_like(low)))
        leaf = lax.broadcasted_iota(jnp.int32, (peers, cols, width), 2) // cols
        names = jnp.zeros((peers, cols, width), F32)
        for k in range(tgt_ref.shape[0]):
            names = jnp.where(leaf == k, tgt_ref[k].astype(F32), names)
        send_ref[...] = jnp.concatenate([mine.reshape(peers, cols, width), names], axis=1).astype(BF16)


def transfer_kernel(c_ref, blocks_ref, after_ref, m_ref, out_ref):
    width = m_ref.shape[1]
    count = m_ref.shape[0]
    ms = []
    for j in range(count):
        inverse = blocks_ref[2 * width * j : 2 * width * j + width, :]
        coupling = blocks_ref[2 * width * j + width : 2 * width * (j + 1), :]
        m = dot_nn(inverse, coupling)
        m_ref[j] = m
        ms.append(m * STEP_SCALE)
    core = c_ref[0]
    blocks = count // CHAIN_BLOCK
    chains = [[-ms[b * CHAIN_BLOCK]] for b in range(blocks)]
    for k in range(1, CHAIN_BLOCK):
        for b in range(blocks):
            chains[b].append(-dot_nn(ms[b * CHAIN_BLOCK + k], chains[b][-1]))
    back = [jnp.zeros((width, width), F32) for _ in range(blocks)]
    for k in reversed(range(CHAIN_BLOCK)):
        shrink = STEP_SCALE ** (2 * (CHAIN_BLOCK - 1 - k))
        for b in range(blocks):
            back[b] = dot_nn(ms[b * CHAIN_BLOCK + k].T, chains[b][k] * shrink - back[b])
    for b in range(blocks):
        carry = chains[b][-1] * (STEP_SCALE**-CHAIN_BLOCK)
        out_ref[width * b : width * (b + 1), :] = jnp.where(core == 0, carry, back[b])


def densify_kernel(plane_size, v_ref, after_ref, d_ref, anc_ref, code_ref, acc_ref):
    sources, rows, width = v_ref.shape
    body = rows - 16
    cols = 8
    lane = lax.broadcasted_iota(jnp.int32, (sources, body), 1)
    tail = v_ref[:, body:rows, :].astype(F32)
    codes = tail[:, cols, :].astype(jnp.int32) * cols + lane % cols
    code_ref[...] = codes.astype(F32).T
    row = lax.broadcasted_iota(jnp.int32, (acc_ref.shape[0], body), 0)
    for s in range(0, sources, 2):
        pick = jnp.concatenate(
            [(row == codes[s + i : s + i + 1, :]).astype(F32).astype(BF16) for i in range(2)], axis=1
        )
        values = v_ref[s : s + 2, 0:body, :].reshape(2 * body, width)
        term = jnp.dot(pick, values, preferred_element_type=F32)
        if s == 0:
            acc_ref[...] = term
        else:
            acc_ref[...] += term
    d_ref[...] = acc_ref[...].astype(BF16).reshape(d_ref.shape)
    per = sources // plane_size
    for j in range(plane_size):
        total = tail[j, 0:cols, :]
        for y in range(1, per):
            total = total + tail[y * plane_size + j, 0:cols, :]
        anc_ref[cols * j : cols * (j + 1), :] = total


def block_solve_kernel(e_ref, anc_ref, blocks_ref, m_ref, b_ref, out_ref):
    count, width = m_ref.shape[0:2]
    cols = anc_ref.shape[0] // count
    total = e_ref[0].astype(F32)
    for z in range(1, e_ref.shape[0]):
        total = total + e_ref[z].astype(F32)
    reduced = anc_ref[...] - total
    bs = []
    for j in range(count):
        inverse = blocks_ref[2 * width * j : 2 * width * j + width, :]
        b = dot_nt(reduced[cols * j : cols * (j + 1)], inverse)
        b_ref[cols * j : cols * (j + 1), :] = b
        bs.append(b)
    blocks = count // CHAIN_BLOCK
    solved = [[bs[b * CHAIN_BLOCK]] for b in range(blocks)]
    for k in range(1, CHAIN_BLOCK):
        for b in range(blocks):
            j = b * CHAIN_BLOCK + k
            solved[b].append(bs[j] - dot_nt(solved[b][-1], m_ref[j]))
    back = [jnp.zeros((cols, width), F32) for _ in range(blocks)]
    for k in reversed(range(CHAIN_BLOCK)):
        for b in range(blocks):
            back[b] = dot_nn(solved[b][k] - back[b], m_ref[b * CHAIN_BLOCK + k])
    ends = jnp.concatenate([solved[b][-1] for b in range(blocks)] + back, axis=0)
    for z in range(out_ref.shape[0]):
        out_ref[z] = ends


def carry_kernel(z_ref, ends_ref, pt_ref, b_ref, blocks_ref, m_ref, x_ref, fine_ref, s_ref, u_ref):
    planes = ends_ref.shape[0]
    count, width = m_ref.shape[0:2]
    cols = b_ref.shape[0] // count
    per = count // CHAIN_BLOCK
    blocks = planes * per
    state = jnp.zeros((cols, width), F32)
    grow = STEP_SCALE ** (-2 * CHAIN_BLOCK)
    back_ends = []
    for j in range(blocks):
        z, b = j // per, j % per
        s_ref[j] = state
        back = ends_ref[z, cols * (per + b) : cols * (per + b + 1), :]
        if j > 0:
            back = back + grow * dot_nt(state, pt_ref[2 * z + 1, width * b : width * (b + 1), :])
        back_ends.append(back)
        if j < blocks - 1:
            leaving = ends_ref[z, cols * b : cols * (b + 1), :]
            if j > 0:
                leaving = leaving + dot_nt(state, pt_ref[2 * z, width * b : width * (b + 1), :])
            state = leaving
    follow = jnp.zeros((cols, width), F32)
    for j in reversed(range(blocks)):
        z, b = j // per, j % per
        u_ref[j] = follow
        if j > 0:
            back = back_ends[j]
            if j < blocks - 1:
                back = back + dot_nn(follow, pt_ref[2 * z, width * b : width * (b + 1), :])
            follow = back
    first = z_ref[0] * per
    solved = [[] for _ in range(per)]
    running = [s_ref[first + b] for b in range(per)]
    for k in range(CHAIN_BLOCK):
        for b in range(per):
            j = b * CHAIN_BLOCK + k
            running[b] = b_ref[cols * j : cols * (j + 1), :] - dot_nt(running[b], m_ref[j])
            solved[b].append(running[b])
    running = [u_ref[first + b] for b in range(per)]
    for k in reversed(range(CHAIN_BLOCK)):
        for b in range(per):
            j = b * CHAIN_BLOCK + k
            right = solved[b][k] - running[b]
            if k > 0:
                running[b] = dot_nn(right, m_ref[j])
            answer = dot_nn(right, blocks_ref[2 * width * j : 2 * width * j + width, :])
            high = answer.astype(BF16).astype(F32)
            fine_ref[j] = jnp.concatenate([high, answer - high], axis=0).astype(BF16)
            s_ref[j] = high
    coarse = s_ref[0:count].reshape(count * cols, width).astype(BF16)
    for z in range(x_ref.shape[0]):
        x_ref[z] = coarse


def choose_kernel(plane_size, x_ref, code_ref, fine_ref, send_ref):
    rows = x_ref.shape[0]
    body = code_ref.shape[0]
    lane = lax.broadcasted_iota(jnp.int32, (body, rows), 1)
    codes = code_ref[...].astype(jnp.int32)
    values = x_ref[...]
    for d in range(send_ref.shape[0]):
        pick = (lane == codes[:, d : d + 1]).astype(F32).astype(BF16)
        send_ref[d, 0:body, :] = jnp.dot(pick, values, preferred_element_type=F32).astype(BF16)
        send_ref[d, body : body + 16, :] = fine_ref[d % plane_size]


def leaf_backward_kernel(w_ref, fwd_ref, inv_ref, upd_ref, out_ref, anc_ref):
    step = pl.program_id(0)
    last = pl.num_programs(0) - 1
    peers, rows, width = w_ref.shape
    cols = rows // 2

    @pl.when(step < last)
    def _():
        came = w_ref[...].astype(F32)
        for k in range(2):
            chosen = came[:, k * cols : (k + 1) * cols, :].reshape(peers * cols, width).astype(BF16)
            correction = jnp.dot(chosen, upd_ref[k], preferred_element_type=F32)
            residue = (fwd_ref[k].astype(F32) - correction).astype(BF16)
            out_ref[k] = lax.dot_general(
                inv_ref[k], residue, (((0,), (1,)), ((), ())), preferred_element_type=F32
            ).astype(BF16)

    @pl.when(step == last)
    def _():
        came = w_ref[...].astype(F32)
        total = came[:, 0:cols, :] + came[:, cols:rows, :]
        anc_ref[...] = total.reshape(peers * cols, width).T


def whole(shape):
    return pl.BlockSpec(shape, lambda *_: (0,) * len(shape))


SMEM = pl.BlockSpec(memory_space=pltpu.SMEM)


def call(kernel, operands, outs, scratch=(), flops=0, after=()):
    moved = sum(a.size * a.dtype.itemsize for a in list(operands) + list(outs))
    return pl.pallas_call(
        kernel,
        out_shape=outs,
        in_specs=[
            SMEM if a.dtype == jnp.int32 else pl.BlockSpec(memory_space=pltpu.VMEM) for a in operands
        ]
        + [pl.BlockSpec(memory_space=pl.ANY) for _ in after],
        out_specs=[pl.BlockSpec(memory_space=pltpu.VMEM) for _ in outs],
        scratch_shapes=list(scratch),
        compiler_params=pltpu.CompilerParams(vmem_limit_bytes=40 * 2**20),
        cost_estimate=pl.CostEstimate(flops=flops, bytes_accessed=moved, transcendentals=0),
    )(*operands, *after)


def local(leaf_rhs, leaf_inverse, leaf_update, leaf_target, anc_rhs, anc_inverse, anc_coupling):
    rhs, inv, upd = leaf_rhs[0], leaf_inverse[0], leaf_update[0]
    leaves, width, rhs_count = rhs.shape
    peers = lax.axis_size(PLANE_AXES)
    planes = lax.axis_size("z")
    plane_size = lax.axis_size(("x", "c"))
    chain = planes * plane_size
    cols = rhs_count // peers
    sds = jax.ShapeDtypeStruct
    y_index, z_index, c_index = (
        lax.axis_index(a).astype(jnp.int32).reshape(1) for a in ("y", "z", "c")
    )

    blocks = lax.all_gather(
        jnp.concatenate([anc_inverse[0], anc_coupling[0]], axis=0), ("x", "c"), axis=0, tiled=True
    )

    targets = leaf_target.astype(jnp.int32).reshape(leaves)
    steps = leaves // 2 + 1
    leaf = lambda i: (jnp.minimum(i, steps - 2), 0, 0)
    forward, send = pl.pallas_call(
        functools.partial(leaf_forward_kernel, peers),
        grid=(steps,),
        out_shape=[
            sds((leaves, rhs_count, width), BF16),
            sds((peers, cols * leaves + 2 * cols, width), BF16),
        ],
        in_specs=[
            SMEM,
            pl.BlockSpec((2, width, rhs_count), leaf),
            pl.BlockSpec((2, width, width), leaf),
            pl.BlockSpec((2, width, width), leaf),
            SMEM,
            whole((width, rhs_count)),
        ],
        out_specs=[
            pl.BlockSpec((2, rhs_count, width), leaf),
            pl.BlockSpec((peers, 2 * cols, width), lambda i: (0, i, 0)),
        ],
        compiler_params=pltpu.CompilerParams(
            dimension_semantics=("arbitrary",), vmem_limit_bytes=40 * 2**20
        ),
    )(y_index, rhs, inv, upd, targets, anc_rhs[0])

    came = lax.all_to_all(send, PLANE_AXES, 0, 0, tiled=True)

    m_blocks, transfer = call(
        transfer_kernel,
        (c_index, blocks),
        [sds((plane_size, width, width), F32), sds((plane_size // CHAIN_BLOCK * width, width), F32)],
        after=(came,),
    )
    transfers = lax.all_gather(transfer, ("z", "c"), axis=0, tiled=True)
    transfers = transfers.reshape((2 * planes,) + transfer.shape)

    dense, anc_rows, codes = call(
        functools.partial(densify_kernel, plane_size),
        (came,),
        [
            sds((planes, plane_size * cols, width), BF16),
            sds((plane_size * cols, width), F32),
            sds((leaves * cols, peers), F32),
        ],
        scratch=[pltpu.VMEM((chain * cols, width), F32)],
        after=(transfer,),
    )
    sums = lax.all_to_all(dense, "z", 0, 0, tiled=True)
    b_rows, ends = call(
        block_solve_kernel,
        (sums, anc_rows, blocks, m_blocks),
        [
            sds((plane_size * cols, width), F32),
            sds((planes, 2 * (plane_size // CHAIN_BLOCK) * cols, width), F32),
        ],
    )
    all_ends = lax.all_to_all(ends, "z", 0, 0, tiled=True)
    per_chain = chain // CHAIN_BLOCK
    x_rows, fine = call(
        carry_kernel,
        (z_index, all_ends, transfers, b_rows, blocks, m_blocks),
        [sds((planes, plane_size * cols, width), BF16), sds((plane_size, 2 * cols, width), BF16)],
        scratch=[
            pltpu.VMEM((max(per_chain, plane_size), cols, width), F32),
            pltpu.VMEM((per_chain, cols, width), F32),
        ],
    )
    all_x = lax.all_to_all(x_rows, "z", 0, 0, tiled=True).reshape(chain * cols, width)
    (answer,) = call(
        functools.partial(choose_kernel, plane_size),
        (all_x, codes, fine),
        [sds(send.shape, BF16)],
    )
    answers = lax.all_to_all(answer, PLANE_AXES, 0, 0, tiled=True)

    leaf_solution, anc_solution = pl.pallas_call(
        leaf_backward_kernel,
        grid=(steps,),
        out_shape=[sds((leaves, width, rhs_count), BF16), sds((width, rhs_count), F32)],
        in_specs=[
            pl.BlockSpec((peers, 2 * cols, width), lambda i: (0, i, 0)),
            pl.BlockSpec((2, rhs_count, width), leaf),
            pl.BlockSpec((2, width, width), leaf),
            pl.BlockSpec((2, width, width), leaf),
        ],
        out_specs=[pl.BlockSpec((2, width, rhs_count), leaf), whole((width, rhs_count))],
        compiler_params=pltpu.CompilerParams(
            dimension_semantics=("arbitrary",), vmem_limit_bytes=40 * 2**20
        ),
    )(answers, forward, inv, upd)
    return (leaf_solution[None], anc_solution[None])


def build(mesh, sizes):
    inner = Mesh(mesh.devices.reshape(sizes), ("y", "z", "x", "c"))
    leaf4 = P("y", ("z", "x", "c"), None, None)
    owner = P(("z", "x", "c"), None, None)
    return jax.shard_map(
        local,
        mesh=inner,
        in_specs=(leaf4, leaf4, leaf4, P("y", ("z", "x", "c"), None), owner, owner, owner),
        out_specs=(leaf4, owner),
        check_vma=False,
    )


def solution(mesh):
    return build(mesh, (4, 8, 4, 2))
```

```python
import functools

import jax
import jax.numpy as jnp
from jax import lax
from jax.experimental import pallas as pl
from jax.experimental.pallas import tpu as pltpu
from jax.sharding import Mesh
from jax.sharding import PartitionSpec as P

F32 = jnp.float32
BF16 = jnp.bfloat16
PLANE_AXES = ("y", "x")
STEP_SCALE = 2.0**-8
CHAIN_BLOCK = 4
COLS = 8
LEAF_STEP = 4


def dot_nn(a, b):
    return lax.dot_general(
        a, b, (((1,), (0,)), ((), ())), precision=lax.Precision.HIGHEST, preferred_element_type=F32
    )


def split(value):
    high = value.astype(BF16)
    return high, (value - high.astype(F32)).astype(BF16)


def rows_by(rows, parts, contract):
    count = rows.shape[0]
    high, low = split(rows)
    dims = (((1,), (contract,)), ((), ()))
    both = jnp.concatenate([high.astype(F32), low.astype(F32)], axis=0).astype(BF16)
    first = lax.dot_general(both, parts[0], dims, preferred_element_type=F32)
    total = first[:count] + first[count:]
    if len(parts) > 1:
        total = total + lax.dot_general(high, parts[1], dims, preferred_element_type=F32)
    return total


def rows_nn(rows, *parts):
    return rows_by(rows, parts, 0)


def rows_nt(rows, *parts):
    return rows_by(rows, parts, 1)


def leaf_forward_kernel(y_ref, tgt_ref, rhs_ref, inv_ref, upd_ref, anc_ref, fwd_ref, send_ref):
    step = pl.program_id(0)
    rhs_count, width = fwd_ref.shape[1:]
    peers = send_ref.shape[0]
    tiles = send_ref.shape[1]
    for pair in range(LEAF_STEP // 2):
        parts = []
        for k in range(2):
            leaf = 2 * pair + k
            forward = lax.dot_general(
                rhs_ref[leaf], inv_ref[leaf], (((0,), (1,)), ((), ())), preferred_element_type=F32
            ).astype(BF16)
            fwd_ref[leaf] = forward
            update = lax.dot_general(
                forward, upd_ref[leaf], (((1,), (1,)), ((), ())), preferred_element_type=F32
            )
            parts.append(update.reshape(peers, 2 * COLS, width))
        for half in range(2):
            rows = jnp.concatenate([p[:, half * COLS : (half + 1) * COLS, :] for p in parts], axis=1)
            send_ref[:, 2 * (step * (LEAF_STEP // 2) + pair) + half] = rows.astype(BF16)

    @pl.when(step == 0)
    def _():
        rows = anc_ref[...].T.reshape(peers, 2 * COLS, width)
        high = rows.astype(BF16).astype(F32)
        layer = y_ref[0]
        mine = jnp.where(layer == 0, high, jnp.where(layer == 2, rows - high, jnp.zeros_like(rows)))
        over = jnp.where(layer == 1, high, jnp.where(layer == 3, rows - high, jnp.zeros_like(rows)))
        mine = mine[:, 0:COLS] + over[:, COLS : 2 * COLS]
        leaf = lax.broadcasted_iota(jnp.int32, (COLS, width), 1) // COLS
        names = jnp.zeros((COLS, width), F32)
        for k in range(tgt_ref.shape[0]):
            names = jnp.where(leaf == k, tgt_ref[k].astype(F32), names)
        names = jnp.broadcast_to(names[None], (peers, COLS, width))
        send_ref[:, tiles - 1] = jnp.concatenate([mine, names], axis=1).astype(BF16)


def own_pair_kernel(inv_ref, cpl_ref, out_ref):
    inverse = inv_ref[0]
    out_ref[0], out_ref[1] = split(dot_nn(inverse, cpl_ref[0]))
    out_ref[2] = inverse.astype(BF16)


def transfer_kernel(x_count, x_ref, c_ref, *refs):
    pairs = refs[: 2 * x_count]
    m_ref, carry_ref, plane_ref = refs[-3:]
    count, _, width = m_ref.shape[0:3]
    x, core = x_ref[0], c_ref[0]
    for d in range(x_count):
        for other in range(2):
            place = 2 * lax.rem(x + d, x_count) + jnp.where(other == 0, core, 1 - core)
            m_ref[place] = pairs[other * x_count + d][...]
    blocks = count // CHAIN_BLOCK

    def scaled(j):
        return (m_ref[j, 0].astype(F32) + m_ref[j, 1].astype(F32)) * STEP_SCALE

    chains = [-scaled(b * CHAIN_BLOCK) for b in range(blocks)]
    for k in range(1, CHAIN_BLOCK):
        for b in range(blocks):
            chains[b] = -dot_nn(scaled(b * CHAIN_BLOCK + k), chains[b])
    total = chains[0]
    for b in range(1, blocks):
        total = dot_nn(chains[b], total)
    for b in range(blocks):
        carry_ref[b, 0], carry_ref[b, 1] = split(chains[b] * (STEP_SCALE**-CHAIN_BLOCK))
    high, low = split(total)
    plane_ref[...] = jnp.where(core == 0, high.astype(F32), low.astype(F32)).astype(BF16)


def densify_kernel(plane_size, z_ref, c_ref, v_ref, keep_ref, give_ref, code_ref, acc_ref):
    sources, tiles, rows, width = v_ref.shape
    planes = keep_ref.shape[0]
    x_count = plane_size // 2
    body = (tiles - 1) // 2 * rows
    lane = lax.broadcasted_iota(jnp.int32, (sources, body), 1)
    last = v_ref[:, tiles - 1].astype(F32)
    codes = last[:, COLS, :].astype(jnp.int32) * COLS + lane % COLS
    code_ref[...] = codes.astype(F32).T
    row = lax.broadcasted_iota(jnp.int32, (acc_ref.shape[1], body), 0)

    def values(s):
        came = v_ref[s, 0 : tiles - 1].reshape((tiles - 1) // 2, 2, rows, width)
        return jnp.concatenate([came[:, half].reshape(body, width) for half in range(2)], axis=1)

    total = None
    for s in range(0, sources, 2):
        pick = jnp.concatenate(
            [(row == codes[s + i : s + i + 1, :]).astype(F32).astype(BF16) for i in range(2)], axis=1
        )
        both = jnp.concatenate([values(s), values(s + 1)], axis=0)
        term = jnp.dot(pick, both, preferred_element_type=F32)
        total = term if total is None else total + term
    for half in range(2):
        acc_ref[half] = -total[:, width * half : width * (half + 1)]
    z, core = z_ref[0], c_ref[0]
    own = pl.multiple_of(z * plane_size * COLS, plane_size * COLS)
    for x in range(x_count):
        for half in range(2):
            mine = last[half * x_count + x, 0:COLS]
            for y in range(half + 2, sources // x_count, 2):
                mine = mine + last[y * x_count + x, 0:COLS]
            place = pl.ds(pl.multiple_of(own + (2 * x + core) * COLS, COLS), COLS)
            acc_ref[half, place, :] += mine
    per = plane_size * COLS
    for z in range(planes):
        keep_ref[z] = acc_ref[core, per * z : per * (z + 1), :]
        give_ref[z] = acc_ref[1 - core, per * z : per * (z + 1), :].astype(BF16)


def block_solve_kernel(e_ref, m_ref, carry_ref, plane_ref, b_ref, mid_ref, out_ref):
    count, _, width = m_ref.shape[0:3]
    reduced = e_ref[0].astype(F32)
    for s in range(1, e_ref.shape[0]):
        reduced = reduced + e_ref[s].astype(F32)
    bs = []
    for j in range(count):
        b = rows_nt(reduced[COLS * j : COLS * (j + 1)], m_ref[j, 2])
        b_ref[COLS * j : COLS * (j + 1), :] = b
        bs.append(b)
    ends = [bs[0], bs[CHAIN_BLOCK]]
    for k in range(1, CHAIN_BLOCK):
        for b in range(2):
            j = b * CHAIN_BLOCK + k
            ends[b] = bs[j] - rows_nt(ends[b], m_ref[j, 0], m_ref[j, 1])
    mid_ref[...] = ends[0]
    leaving = ends[1] + rows_nt(ends[0], carry_ref[1, 0], carry_ref[1, 1])
    high, low = split(leaving)
    ends = jnp.concatenate([high.astype(F32), low.astype(F32)], axis=0).astype(BF16)
    for z in range(out_ref.shape[0]):
        out_ref[z, 0 : 2 * COLS] = ends
        out_ref[z, 2 * COLS : 2 * COLS + width] = plane_ref[...]


def carry_forward_kernel(
    z_ref, c_ref, ends_ref, other_ref, b_ref, mid_ref, m_ref, carry_ref, s_ref, back_ref, flow_ref, phi_ref
):
    planes = ends_ref.shape[0]
    width = m_ref.shape[2]
    core = c_ref[0]
    for z in range(planes):
        phi_ref[z, core] = ends_ref[z, 2 * COLS : 2 * COLS + width]
        phi_ref[z, 1 - core] = other_ref[z, 2 * COLS : 2 * COLS + width]
    grow = STEP_SCALE ** (-2 * CHAIN_BLOCK)
    own = z_ref[0]
    state = jnp.zeros((COLS, width), F32)
    flow = state
    for z in range(planes - 1):
        parts = ends_ref[z, 0 : 2 * COLS].astype(F32)
        leaving = parts[0:COLS] + parts[COLS : 2 * COLS]
        if z > 0:
            leaving = leaving + grow * rows_nt(state, phi_ref[z, 0], phi_ref[z, 1])
        state = leaving
        flow = jnp.where(own == z + 1, state, flow)
    running = [flow, mid_ref[...] + rows_nt(flow, carry_ref[0, 0], carry_ref[0, 1])]
    solved = [[], []]
    for k in range(CHAIN_BLOCK):
        for b in range(2):
            j = b * CHAIN_BLOCK + k
            running[b] = b_ref[COLS * j : COLS * (j + 1), :] - rows_nt(running[b], m_ref[j, 0], m_ref[j, 1])
            s_ref[COLS * j : COLS * (j + 1), :] = running[b]
            solved[b].append(running[b])
    back = [None, None]
    for k in reversed(range(CHAIN_BLOCK)):
        for b in range(2):
            j = b * CHAIN_BLOCK + k
            right = solved[b][k] if back[b] is None else solved[b][k] - back[b]
            back[b] = rows_nn(right, m_ref[j, 0], m_ref[j, 1])
    flow_ref[...] = back[1]
    leaving = back[0] + rows_nn(back[1], carry_ref[0, 0], carry_ref[0, 1])
    for z in range(back_ref.shape[0]):
        back_ref[z] = leaving


def carry_backward_kernel(z_ref, ends_ref, phi_ref, s_ref, flow_ref, m_ref, carry_ref, x_ref):
    planes = ends_ref.shape[0]
    count, _, width = m_ref.shape[0:3]
    grow = STEP_SCALE ** (-2 * CHAIN_BLOCK)
    own = z_ref[0]
    state = jnp.zeros((COLS, width), F32)
    flow = state
    for z in reversed(range(1, planes)):
        leaving = ends_ref[z]
        if z < planes - 1:
            leaving = leaving + grow * rows_nn(state, phi_ref[z, 0], phi_ref[z, 1])
        state = leaving
        flow = jnp.where(own == z - 1, state, flow)
    running = [flow_ref[...] + rows_nn(flow, carry_ref[1, 0], carry_ref[1, 1]), flow]
    answers = [None] * count
    for k in reversed(range(CHAIN_BLOCK)):
        for b in range(2):
            j = b * CHAIN_BLOCK + k
            right = s_ref[COLS * j : COLS * (j + 1), :] - running[b]
            if k > 0:
                running[b] = rows_nn(right, m_ref[j, 0], m_ref[j, 1])
            answers[j] = rows_nn(right, m_ref[j, 2])
    coarse = jnp.concatenate(answers, axis=0).astype(BF16)
    for z in range(x_ref.shape[0]):
        x_ref[z] = coarse


def choose_kernel(plane_size, z_ref, c_ref, x_ref, other_ref, code_ref, send_ref):
    peers, tiles, rows, width = send_ref.shape
    planes = x_ref.shape[0]
    body = code_ref.shape[0]
    core = c_ref[0]
    lane = lax.broadcasted_iota(jnp.int32, (body, planes * plane_size * COLS), 1)
    codes = code_ref[...].astype(jnp.int32)
    x_count = plane_size // 2
    mine, theirs = x_ref[...].astype(F32), other_ref[...].astype(F32)
    halves = [jnp.where(core == half, mine, theirs).reshape(lane.shape[1], width) for half in range(2)]
    values = jnp.concatenate(halves, axis=1).astype(BF16)
    mine, theirs = x_ref[z_ref[0]].astype(F32), other_ref[z_ref[0]].astype(F32)
    own = [jnp.where(core == half, mine, theirs) for half in range(2)]
    for d in range(peers):
        pick = (lane == codes[:, d : d + 1]).astype(F32).astype(BF16)
        chosen = jnp.dot(pick, values, preferred_element_type=F32).astype(BF16)
        for half in range(2):
            part = chosen[:, width * half : width * (half + 1)].reshape(body // rows, rows, width)
            for pair in range(body // rows):
                send_ref[d, 2 * pair + half] = part[pair]
        j = 2 * (d % x_count)
        ends = [
            jnp.where(
                core == 0, own[half][COLS * j : COLS * (j + 1)], own[half][COLS * (j + 1) : COLS * (j + 2)]
            )
            for half in range(2)
        ]
        send_ref[d, tiles - 1] = jnp.concatenate(ends, axis=0).astype(BF16)


def leaf_backward_kernel(w_ref, tail_ref, fwd_ref, inv_ref, upd_ref, out_ref, anc_ref):
    step = pl.program_id(0)
    peers, _, rows, width = w_ref.shape
    rhs_count = fwd_ref.shape[1]
    for pair in range(LEAF_STEP // 2):
        came = [w_ref[:, 2 * pair + half].astype(F32) for half in range(2)]
        for k in range(2):
            leaf = 2 * pair + k
            both = jnp.concatenate([c[:, k * COLS : (k + 1) * COLS, :] for c in came], axis=1)
            chosen = both.reshape(rhs_count, width).astype(BF16)
            correction = jnp.dot(chosen, upd_ref[leaf], preferred_element_type=F32)
            residue = (fwd_ref[leaf].astype(F32) - correction).astype(BF16)
            out_ref[leaf] = lax.dot_general(
                inv_ref[leaf], residue, (((0,), (1,)), ((), ())), preferred_element_type=F32
            ).astype(BF16)

    @pl.when(step == 0)
    def _():
        anc_ref[...] = tail_ref[:, 0].astype(F32).reshape(rhs_count, width).T


SMEM = pl.BlockSpec(memory_space=pltpu.SMEM)


def call(kernel, operands, outs, scratch=(), flops=0, after=()):
    moved = sum(a.size * a.dtype.itemsize for a in list(operands) + list(outs))
    if after:
        inner, count = kernel, len(operands)
        kernel = lambda *refs: inner(*refs[:count], *refs[count + len(after) :])
    return pl.pallas_call(
        kernel,
        out_shape=outs,
        in_specs=[
            SMEM if a.dtype == jnp.int32 else pl.BlockSpec(memory_space=pltpu.VMEM) for a in operands
        ]
        + [pl.BlockSpec(memory_space=pl.ANY) for _ in after],
        out_specs=[pl.BlockSpec(memory_space=pltpu.VMEM) for _ in outs],
        scratch_shapes=list(scratch),
        compiler_params=pltpu.CompilerParams(vmem_limit_bytes=16 * 2**20),
        cost_estimate=pl.CostEstimate(flops=flops, bytes_accessed=moved, transcendentals=0),
    )(*operands, *after)


def shift(value, axis, by):
    size = lax.axis_size(axis)
    return lax.ppermute(value, axis, [((i + by) % size, i) for i in range(size)])


def local(leaf_rhs, leaf_inverse, leaf_update, leaf_target, anc_rhs, anc_inverse, anc_coupling):
    rhs, inv, upd = leaf_rhs[0], leaf_inverse[0], leaf_update[0]
    leaves, width, rhs_count = rhs.shape
    peers = lax.axis_size(PLANE_AXES)
    planes = lax.axis_size("z")
    x_count = lax.axis_size("x")
    plane_size = 2 * x_count
    chain = planes * plane_size
    pairs = leaves // 2
    sds = jax.ShapeDtypeStruct
    y_index, z_index, x_index, c_index = (
        lax.axis_index(a).astype(jnp.int32).reshape(1) for a in ("y", "z", "x", "c")
    )

    (own_pair,) = call(own_pair_kernel, (anc_inverse, anc_coupling), [sds((3, width, width), BF16)])
    along = [own_pair] + [shift(own_pair, "x", d) for d in range(1, x_count)]

    steps = leaves // LEAF_STEP
    leaf = lambda i: (i, 0, 0)
    forward, send = pl.pallas_call(
        leaf_forward_kernel,
        grid=(steps,),
        out_shape=[
            sds((leaves, rhs_count, width), BF16),
            sds((peers, 2 * pairs + 1, 2 * COLS, width), BF16),
        ],
        in_specs=[
            SMEM,
            SMEM,
            pl.BlockSpec((LEAF_STEP, width, rhs_count), leaf),
            pl.BlockSpec((LEAF_STEP, width, width), leaf),
            pl.BlockSpec((LEAF_STEP, width, width), leaf),
            pl.BlockSpec((width, rhs_count), lambda i: (0, 0)),
        ],
        out_specs=[
            pl.BlockSpec((LEAF_STEP, rhs_count, width), leaf),
            pl.BlockSpec((peers, 2 * pairs + 1, 2 * COLS, width), lambda i: (0, 0, 0, 0)),
        ],
        compiler_params=pltpu.CompilerParams(
            dimension_semantics=("arbitrary",), vmem_limit_bytes=60 * 2**20
        ),
    )(y_index, leaf_target.astype(jnp.int32).reshape(leaves), rhs, inv, upd, anc_rhs[0])

    send, *along = lax.optimization_barrier((send, *along))
    came = lax.all_to_all(send, PLANE_AXES, 0, 0, tiled=True)

    across = [shift(pair, "c", 1) for pair in along]
    m_blocks, carries, plane_carry = call(
        functools.partial(transfer_kernel, x_count),
        (x_index, c_index, *along, *across),
        [
            sds((plane_size, 3, width, width), BF16),
            sds((2, 2, width, width), BF16),
            sds((width, width), BF16),
        ],
    )

    keep, give, codes = call(
        functools.partial(densify_kernel, plane_size),
        (z_index, c_index, came),
        [
            sds((planes, plane_size * COLS, width), F32),
            sds((planes, plane_size * COLS, width), BF16),
            sds((leaves * COLS, peers), F32),
        ],
        scratch=[pltpu.VMEM((2, chain * COLS, width), F32)],
        after=(plane_carry,),
    )
    dense = (keep + shift(give, "c", 1).astype(F32)).astype(BF16)
    sums = lax.all_to_all(dense, "z", 0, 0, tiled=True)
    b_rows, middle, ends = call(
        block_solve_kernel,
        (sums, m_blocks, carries, plane_carry),
        [
            sds((plane_size * COLS, width), F32),
            sds((COLS, width), F32),
            sds((planes, 2 * COLS + width, width), BF16),
        ],
    )
    all_ends = lax.all_to_all(ends, "z", 0, 0, tiled=True)
    other_ends = shift(all_ends, "c", 1)
    s_rows, back, flow, phis = call(
        carry_forward_kernel,
        (z_index, c_index, all_ends, other_ends, b_rows, middle, m_blocks, carries),
        [
            sds((plane_size * COLS, width), F32),
            sds((planes, COLS, width), F32),
            sds((COLS, width), F32),
            sds((planes, 2, width, width), BF16),
        ],
    )
    all_back = lax.all_to_all(back, "z", 0, 0, tiled=True)
    (x_rows,) = call(
        carry_backward_kernel,
        (z_index, all_back, phis, s_rows, flow, m_blocks, carries),
        [sds((planes, plane_size * COLS, width), BF16)],
    )
    all_x = lax.all_to_all(x_rows, "z", 0, 0, tiled=True)
    other_x = shift(all_x, "c", 1)
    (answer,) = call(
        functools.partial(choose_kernel, plane_size),
        (z_index, c_index, all_x, other_x, codes),
        [sds((peers, 2 * pairs + 1, 2 * COLS, width), BF16)],
    )
    answers = lax.all_to_all(answer, PLANE_AXES, 0, 0, tiled=True)

    leaf_solution, anc_solution = pl.pallas_call(
        leaf_backward_kernel,
        grid=(steps,),
        out_shape=[sds((leaves, width, rhs_count), BF16), sds((width, rhs_count), F32)],
        in_specs=[
            pl.BlockSpec((peers, LEAF_STEP, 2 * COLS, width), lambda i: (0, i, 0, 0)),
            pl.BlockSpec((peers, 1, 2 * COLS, width), lambda i: (0, 2 * pairs, 0, 0)),
            pl.BlockSpec((LEAF_STEP, rhs_count, width), leaf),
            pl.BlockSpec((LEAF_STEP, width, width), leaf),
            pl.BlockSpec((LEAF_STEP, width, width), leaf),
        ],
        out_specs=[
            pl.BlockSpec((LEAF_STEP, width, rhs_count), leaf),
            pl.BlockSpec((width, rhs_count), lambda i: (0, 0)),
        ],
        compiler_params=pltpu.CompilerParams(
            dimension_semantics=("arbitrary",), vmem_limit_bytes=40 * 2**20
        ),
    )(answers, answers, forward, inv, upd)
    return (leaf_solution[None], anc_solution[None])


def build(mesh, sizes):
    inner = Mesh(mesh.devices.reshape(sizes), ("y", "z", "x", "c"))
    leaf4 = P("y", ("z", "x", "c"), None, None)
    owner = P(("z", "x", "c"), None, None)
    return jax.shard_map(
        local,
        mesh=inner,
        in_specs=(leaf4, leaf4, leaf4, P("y", ("z", "x", "c"), None), owner, owner, owner),
        out_specs=(leaf4, owner),
        check_vma=False,
    )


def solution(mesh):
    return build(mesh, (4, 8, 4, 2))
```

```python
import functools

import jax
import jax.numpy as jnp
from jax import lax
from jax.experimental import pallas as pl
from jax.experimental.pallas import tpu as pltpu
from jax.sharding import Mesh
from jax.sharding import PartitionSpec as P

F32 = jnp.float32
BF16 = jnp.bfloat16
PLANE_AXES = ("y", "x")
STEP_SCALE = 2.0**-8
COLS = 8
LEAF_STEP = 4


def dot_nn(a, b):
    return lax.dot_general(
        a, b, (((1,), (0,)), ((), ())), precision=lax.Precision.HIGHEST, preferred_element_type=F32
    )


def split(value):
    high = value.astype(BF16)
    return high, (value - high.astype(F32)).astype(BF16)


def rows_by(rows, parts, contract):
    count = rows.shape[0]
    high, low = split(rows)
    dims = (((1,), (contract,)), ((), ()))
    both = jnp.concatenate([high.astype(F32), low.astype(F32)], axis=0).astype(BF16)
    first = lax.dot_general(both, parts[0], dims, preferred_element_type=F32)
    total = first[:count] + first[count:]
    if len(parts) > 1:
        total = total + lax.dot_general(high, parts[1], dims, preferred_element_type=F32)
    return total


def rows_nn(rows, *parts):
    return rows_by(rows, parts, 0)


def rows_nt(rows, *parts):
    return rows_by(rows, parts, 1)


def leaf_forward_kernel(y_ref, tgt_ref, rhs_ref, inv_ref, upd_ref, anc_ref, fwd_ref, send_ref):
    step = pl.program_id(0)
    rhs_count, width = fwd_ref.shape[1:]
    peers = send_ref.shape[0]
    tiles = send_ref.shape[1]
    for pair in range(LEAF_STEP // 2):
        parts = []
        for k in range(2):
            leaf = 2 * pair + k
            forward = lax.dot_general(
                rhs_ref[leaf], inv_ref[leaf], (((0,), (1,)), ((), ())), preferred_element_type=F32
            ).astype(BF16)
            fwd_ref[leaf] = forward
            update = lax.dot_general(
                forward, upd_ref[leaf], (((1,), (1,)), ((), ())), preferred_element_type=F32
            )
            parts.append(update.reshape(peers, 2 * COLS, width))
        for half in range(2):
            rows = jnp.concatenate([p[:, half * COLS : (half + 1) * COLS, :] for p in parts], axis=1)
            send_ref[:, 2 * (step * (LEAF_STEP // 2) + pair) + half] = rows.astype(BF16)

    @pl.when(step == 0)
    def _():
        rows = anc_ref[...].T.reshape(peers, 2 * COLS, width)
        high = rows.astype(BF16).astype(F32)
        layer = y_ref[0]
        mine = jnp.where(layer == 0, high, jnp.where(layer == 2, rows - high, jnp.zeros_like(rows)))
        over = jnp.where(layer == 1, high, jnp.where(layer == 3, rows - high, jnp.zeros_like(rows)))
        mine = mine[:, 0:COLS] + over[:, COLS : 2 * COLS]
        leaf = lax.broadcasted_iota(jnp.int32, (COLS, width), 1) // COLS
        names = jnp.zeros((COLS, width), F32)
        for k in range(tgt_ref.shape[0]):
            names = jnp.where(leaf == k, tgt_ref[k].astype(F32), names)
        names = jnp.broadcast_to(names[None], (peers, COLS, width))
        send_ref[:, tiles - 1] = jnp.concatenate([mine, names], axis=1).astype(BF16)


def own_pair_kernel(inv_ref, cpl_ref, out_ref):
    inverse = inv_ref[0]
    out_ref[0], out_ref[1] = split(dot_nn(inverse, cpl_ref[0]))
    out_ref[2] = inverse.astype(BF16)


def transfer_kernel(x_count, x_ref, c_ref, *refs):
    pairs = refs[: 2 * x_count]
    m_ref, pack_ref, top_ref = refs[-3:]
    count, _, width = m_ref.shape[0:3]
    x, core = x_ref[0], c_ref[0]
    for d in range(x_count):
        for other in range(2):
            place = 2 * lax.rem(x + d, x_count) + jnp.where(other == 0, core, 1 - core)
            m_ref[place] = pairs[other * x_count + d][...]
    half = count // 2
    runs = []
    for k in range(count):
        m = (m_ref[k, 0].astype(F32) + m_ref[k, 1].astype(F32)) * STEP_SCALE
        runs.append(-m if k % half == 0 else -dot_nn(m, runs[-1]))
    first = jnp.concatenate(
        [runs[k] * STEP_SCALE ** (count - 1 - k) for k in range(half)], axis=0
    )
    second = jnp.concatenate(
        [runs[k] * STEP_SCALE ** (count - 1 - k) for k in range(half, count)], axis=0
    )
    second = dot_nn(second, runs[half - 1])
    stack = jnp.concatenate([first, second], axis=0)
    top = jnp.maximum(jnp.max(jnp.abs(stack)), 1e-30)
    high, low = split((stack / top).T)
    gram = lax.dot_general(high, high, (((1,), (1,)), ((), ())), preferred_element_type=F32)
    cross = lax.dot_general(high, low, (((1,), (1,)), ((), ())), preferred_element_type=F32)
    pack_ref[0], pack_ref[1] = split(stack[width * (count - 1) :])
    pack_ref[2] = (gram + (cross + cross.T)).astype(BF16)
    top_ref[...] = jnp.full(top_ref.shape, top, F32)


def order_kernel(z_ref, *refs):
    out_ref = refs[-1]
    count = out_ref.shape[0]
    for d in range(count):
        out_ref[lax.rem(z_ref[0] // 2 + d, count)] = refs[d][...]


def densify_kernel(plane_size, z_ref, c_ref, v_ref, keep_ref, give_ref, code_ref, acc_ref):
    sources, tiles, rows, width = v_ref.shape
    planes = keep_ref.shape[0]
    x_count = plane_size // 2
    body = (tiles - 1) // 2 * rows
    lane = lax.broadcasted_iota(jnp.int32, (sources, body), 1)
    last = v_ref[:, tiles - 1].astype(F32)
    codes = last[:, COLS, :].astype(jnp.int32) * COLS + lane % COLS
    code_ref[...] = codes.astype(F32).T
    row = lax.broadcasted_iota(jnp.int32, (acc_ref.shape[1], body), 0)

    def values(s):
        came = v_ref[s, 0 : tiles - 1].reshape((tiles - 1) // 2, 2, rows, width)
        return jnp.concatenate([came[:, half].reshape(body, width) for half in range(2)], axis=1)

    total = None
    for s in range(0, sources, 2):
        pick = jnp.concatenate(
            [(row == codes[s + i : s + i + 1, :]).astype(F32).astype(BF16) for i in range(2)], axis=1
        )
        both = jnp.concatenate([values(s), values(s + 1)], axis=0)
        term = jnp.dot(pick, both, preferred_element_type=F32)
        total = term if total is None else total + term
    for half in range(2):
        acc_ref[half] = -total[:, width * half : width * (half + 1)]
    z, core = z_ref[0], c_ref[0]
    own = pl.multiple_of(z * plane_size * COLS, plane_size * COLS)
    for x in range(x_count):
        for half in range(2):
            mine = last[half * x_count + x, 0:COLS]
            for y in range(half + 2, sources // x_count, 2):
                mine = mine + last[y * x_count + x, 0:COLS]
            place = pl.ds(pl.multiple_of(own + (2 * x + core) * COLS, COLS), COLS)
            acc_ref[half, place, :] += mine
    per = plane_size * COLS
    for z in range(planes):
        keep_ref[z] = acc_ref[core, per * z : per * (z + 1), :]
        give_ref[z] = acc_ref[1 - core, per * z : per * (z + 1), :].astype(BF16)


def block_solve_kernel(e_ref, m_ref, top_ref, b_ref, out_ref):
    count = m_ref.shape[0]
    reduced = e_ref[0].astype(F32)
    for s in range(1, e_ref.shape[0]):
        reduced = reduced + e_ref[s].astype(F32)
    solved = []
    for j in range(count):
        b = rows_nt(reduced[COLS * j : COLS * (j + 1)], m_ref[j, 2])
        b_ref[COLS * j : COLS * (j + 1), :] = b
        if j > 0:
            b = b - rows_nt(solved[-1], m_ref[j, 0], m_ref[j, 1])
        solved.append(b)
    back = rows_nn(solved[-1], m_ref[count - 1, 0], m_ref[count - 1, 1])
    for j in reversed(range(count - 1)):
        back = rows_nn(solved[j] - back, m_ref[j, 0], m_ref[j, 1])
    ends = jnp.concatenate([solved[-1], back, top_ref[...]], axis=0)
    for z in range(out_ref.shape[0]):
        out_ref[z] = ends


def carry_kernel(z_ref, c_ref, ends_ref, mine_ref, other_ref, b_ref, m_ref, x_ref, pack_ref):
    planes = ends_ref.shape[0]
    count, _, width = m_ref.shape[0:3]
    core = c_ref[0]
    for i in range(planes // 2):
        pack_ref[2 * i + core] = mine_ref[i]
        pack_ref[2 * i + 1 - core] = other_ref[i]
    grow = STEP_SCALE**-count
    half_grow = STEP_SCALE ** (-count // 2)
    own = z_ref[0]
    state = jnp.zeros((COLS, width), F32)
    inflow = state
    backs = []
    for z in range(planes):
        leaving, back, top = (ends_ref[z, COLS * i : COLS * (i + 1)] for i in range(3))
        if z > 0:
            answer = rows_nn(state, pack_ref[z, 2])
            for _ in range(2):
                answer = (answer * half_grow) * top * half_grow
            back = back - answer
            leaving = leaving + grow * rows_nt(state, pack_ref[z, 0], pack_ref[z, 1])
        backs.append(back)
        state = leaving
        if z < planes - 1:
            inflow = jnp.where(own == z + 1, state, inflow)
    state = jnp.zeros((COLS, width), F32)
    running = state
    for z in reversed(range(1, planes)):
        leaving = backs[z]
        if z < planes - 1:
            leaving = leaving + grow * rows_nn(state, pack_ref[z, 0], pack_ref[z, 1])
        state = leaving
        running = jnp.where(own == z - 1, state, running)
    solved = []
    for j in range(count):
        inflow = b_ref[COLS * j : COLS * (j + 1), :] - rows_nt(inflow, m_ref[j, 0], m_ref[j, 1])
        solved.append(inflow)
    answers = [None] * count
    for j in reversed(range(count)):
        right = solved[j] - running
        if j > 0:
            running = rows_nn(right, m_ref[j, 0], m_ref[j, 1])
        answers[j] = rows_nn(right, m_ref[j, 2])
    coarse = jnp.concatenate(answers, axis=0).astype(BF16)
    for z in range(x_ref.shape[0]):
        x_ref[z] = coarse


def choose_kernel(plane_size, z_ref, c_ref, x_ref, other_ref, code_ref, send_ref):
    peers, tiles, rows, width = send_ref.shape
    planes = x_ref.shape[0]
    body = code_ref.shape[0]
    core = c_ref[0]
    lane = lax.broadcasted_iota(jnp.int32, (body, planes * plane_size * COLS), 1)
    codes = code_ref[...].astype(jnp.int32)
    x_count = plane_size // 2
    mine, theirs = x_ref[...].astype(F32), other_ref[...].astype(F32)
    halves = [jnp.where(core == half, mine, theirs).reshape(lane.shape[1], width) for half in range(2)]
    values = jnp.concatenate(halves, axis=1).astype(BF16)
    mine, theirs = x_ref[z_ref[0]].astype(F32), other_ref[z_ref[0]].astype(F32)
    own = [jnp.where(core == half, mine, theirs) for half in range(2)]
    for d in range(peers):
        pick = (lane == codes[:, d : d + 1]).astype(F32).astype(BF16)
        chosen = jnp.dot(pick, values, preferred_element_type=F32).astype(BF16)
        for half in range(2):
            part = chosen[:, width * half : width * (half + 1)].reshape(body // rows, rows, width)
            for pair in range(body // rows):
                send_ref[d, 2 * pair + half] = part[pair]
        j = 2 * (d % x_count)
        ends = [
            jnp.where(
                core == 0, own[half][COLS * j : COLS * (j + 1)], own[half][COLS * (j + 1) : COLS * (j + 2)]
            )
            for half in range(2)
        ]
        send_ref[d, tiles - 1] = jnp.concatenate(ends, axis=0).astype(BF16)


def leaf_backward_kernel(w_ref, tail_ref, fwd_ref, inv_ref, upd_ref, out_ref, anc_ref):
    step = pl.program_id(0)
    peers, _, rows, width = w_ref.shape
    rhs_count = fwd_ref.shape[1]
    for pair in range(LEAF_STEP // 2):
        came = [w_ref[:, 2 * pair + half].astype(F32) for half in range(2)]
        for k in range(2):
            leaf = 2 * pair + k
            both = jnp.concatenate([c[:, k * COLS : (k + 1) * COLS, :] for c in came], axis=1)
            chosen = both.reshape(rhs_count, width).astype(BF16)
            correction = jnp.dot(chosen, upd_ref[leaf], preferred_element_type=F32)
            residue = (fwd_ref[leaf].astype(F32) - correction).astype(BF16)
            out_ref[leaf] = lax.dot_general(
                inv_ref[leaf], residue, (((0,), (1,)), ((), ())), preferred_element_type=F32
            ).astype(BF16)

    @pl.when(step == 0)
    def _():
        anc_ref[...] = tail_ref[:, 0].astype(F32).reshape(rhs_count, width).T


SMEM = pl.BlockSpec(memory_space=pltpu.SMEM)


def call(kernel, operands, outs, scratch=(), flops=0, after=(), vmem=16):
    moved = sum(a.size * a.dtype.itemsize for a in list(operands) + list(outs))
    if after:
        inner, count = kernel, len(operands)
        kernel = lambda *refs: inner(*refs[:count], *refs[count + len(after) :])
    return pl.pallas_call(
        kernel,
        out_shape=outs,
        in_specs=[
            SMEM if a.dtype == jnp.int32 else pl.BlockSpec(memory_space=pltpu.VMEM) for a in operands
        ]
        + [pl.BlockSpec(memory_space=pl.ANY) for _ in after],
        out_specs=[pl.BlockSpec(memory_space=pltpu.VMEM) for _ in outs],
        scratch_shapes=list(scratch),
        compiler_params=pltpu.CompilerParams(vmem_limit_bytes=vmem * 2**20),
        cost_estimate=pl.CostEstimate(flops=flops, bytes_accessed=moved, transcendentals=0),
    )(*operands, *after)


def shift(value, axis, by):
    size = lax.axis_size(axis)
    return lax.ppermute(value, axis, [((i + by) % size, i) for i in range(size)])


def every_other(value, by):
    half = lax.axis_size("z") // 2
    return lax.ppermute(
        value,
        ("z", "c"),
        [
            (2 * (2 * ((z // 2 + by) % half) + c) + z % 2, 2 * z + c)
            for z in range(2 * half)
            for c in range(2)
        ],
    )


def local(leaf_rhs, leaf_inverse, leaf_update, leaf_target, anc_rhs, anc_inverse, anc_coupling):
    rhs, inv, upd = leaf_rhs[0], leaf_inverse[0], leaf_update[0]
    leaves, width, rhs_count = rhs.shape
    peers = lax.axis_size(PLANE_AXES)
    planes = lax.axis_size("z")
    x_count = lax.axis_size("x")
    plane_size = 2 * x_count
    chain = planes * plane_size
    pairs = leaves // 2
    sds = jax.ShapeDtypeStruct
    y_index, z_index, x_index, c_index = (
        lax.axis_index(a).astype(jnp.int32).reshape(1) for a in ("y", "z", "x", "c")
    )

    (own_pair,) = call(own_pair_kernel, (anc_inverse, anc_coupling), [sds((3, width, width), BF16)], vmem=60)
    along = [own_pair] + [shift(own_pair, "x", d) for d in range(1, x_count)]

    steps = leaves // LEAF_STEP
    leaf = lambda i: (i, 0, 0)
    forward, send = pl.pallas_call(
        leaf_forward_kernel,
        grid=(steps,),
        out_shape=[
            sds((leaves, rhs_count, width), BF16),
            sds((peers, 2 * pairs + 1, 2 * COLS, width), BF16),
        ],
        in_specs=[
            SMEM,
            SMEM,
            pl.BlockSpec((LEAF_STEP, width, rhs_count), leaf),
            pl.BlockSpec((LEAF_STEP, width, width), leaf),
            pl.BlockSpec((LEAF_STEP, width, width), leaf),
            pl.BlockSpec((width, rhs_count), lambda i: (0, 0)),
        ],
        out_specs=[
            pl.BlockSpec((LEAF_STEP, rhs_count, width), leaf),
            pl.BlockSpec((peers, 2 * pairs + 1, 2 * COLS, width), lambda i: (0, 0, 0, 0)),
        ],
        compiler_params=pltpu.CompilerParams(
            dimension_semantics=("arbitrary",), vmem_limit_bytes=60 * 2**20
        ),
    )(y_index, leaf_target.astype(jnp.int32).reshape(leaves), rhs, inv, upd, anc_rhs[0])

    send, *along = lax.optimization_barrier((send, *along))
    came = lax.all_to_all(send.reshape(peers, -1, width), PLANE_AXES, 0, 0, tiled=True).reshape(send.shape)

    across = [shift(pair, "c", 1) for pair in along]
    m_blocks, pack, top = call(
        functools.partial(transfer_kernel, x_count),
        (x_index, c_index, *along, *across),
        [
            sds((plane_size, 3, width, width), BF16),
            sds((3, width, width), BF16),
            sds((COLS, width), F32),
        ],
    )
    packs = [every_other(pack, d) for d in range(planes // 2)]
    came, *packs = lax.optimization_barrier((came, *packs))

    keep, give, codes = call(
        functools.partial(densify_kernel, plane_size),
        (z_index, c_index, came),
        [
            sds((planes, plane_size * COLS, width), F32),
            sds((planes, plane_size * COLS, width), BF16),
            sds((leaves * COLS, peers), F32),
        ],
        scratch=[pltpu.VMEM((2, chain * COLS, width), F32)],
    )
    dense = (keep + shift(give, "c", 1).astype(F32)).astype(BF16)
    sums = lax.all_to_all(dense, "z", 0, 0, tiled=True)
    (own_packs,) = call(order_kernel, (z_index, *packs), [sds((planes // 2, 3, width, width), BF16)])
    other_packs = shift(own_packs, "c", 1)
    b_rows, ends = call(
        block_solve_kernel,
        (sums, m_blocks, top),
        [sds((plane_size * COLS, width), F32), sds((planes, 3 * COLS, width), F32)],
    )
    all_ends = lax.all_to_all(ends, "z", 0, 0, tiled=True)
    (x_rows,) = call(
        carry_kernel,
        (z_index, c_index, all_ends, own_packs, other_packs, b_rows, m_blocks),
        [sds((planes, plane_size * COLS, width), BF16)],
        scratch=[pltpu.VMEM((planes, 3, width, width), BF16)],
    )
    all_x = lax.all_to_all(x_rows, "z", 0, 0, tiled=True)
    other_x = shift(all_x, "c", 1)
    (answer,) = call(
        functools.partial(choose_kernel, plane_size),
        (z_index, c_index, all_x, other_x, codes),
        [sds((peers, 2 * pairs + 1, 2 * COLS, width), BF16)],
    )
    answers = lax.all_to_all(answer.reshape(peers, -1, width), PLANE_AXES, 0, 0, tiled=True)
    answers = answers.reshape(answer.shape)

    leaf_solution, anc_solution = pl.pallas_call(
        leaf_backward_kernel,
        grid=(steps,),
        out_shape=[sds((leaves, width, rhs_count), BF16), sds((width, rhs_count), F32)],
        in_specs=[
            pl.BlockSpec((peers, LEAF_STEP, 2 * COLS, width), lambda i: (0, i, 0, 0)),
            pl.BlockSpec((peers, 1, 2 * COLS, width), lambda i: (0, 2 * pairs, 0, 0)),
            pl.BlockSpec((LEAF_STEP, rhs_count, width), leaf),
            pl.BlockSpec((LEAF_STEP, width, width), leaf),
            pl.BlockSpec((LEAF_STEP, width, width), leaf),
        ],
        out_specs=[
            pl.BlockSpec((LEAF_STEP, width, rhs_count), leaf),
            pl.BlockSpec((width, rhs_count), lambda i: (0, 0)),
        ],
        compiler_params=pltpu.CompilerParams(
            dimension_semantics=("arbitrary",), vmem_limit_bytes=40 * 2**20
        ),
    )(answers, answers, forward, inv, upd)
    return (leaf_solution[None], anc_solution[None])


def build(mesh, sizes):
    inner = Mesh(mesh.devices.reshape(sizes), ("y", "z", "x", "c"))
    leaf4 = P("y", ("z", "x", "c"), None, None)
    owner = P(("z", "x", "c"), None, None)
    return jax.shard_map(
        local,
        mesh=inner,
        in_specs=(leaf4, leaf4, leaf4, P("y", ("z", "x", "c"), None), owner, owner, owner),
        out_specs=(leaf4, owner),
        check_vma=False,
    )


def solution(mesh):
    return build(mesh, (4, 8, 4, 2))
```

```python
import functools

import jax
import jax.numpy as jnp
from jax import lax
from jax.experimental import pallas as pl
from jax.experimental.pallas import tpu as pltpu
from jax.sharding import Mesh
from jax.sharding import PartitionSpec as P

F32 = jnp.float32
BF16 = jnp.bfloat16
PLANE_AXES = ("y", "x")
CORE_AXES = ("y", "x", "c")
STEP_SCALE = 2.0**-8
COLS = 8
LEAF_STEP = 8


def dot_nn(a, b):
    return lax.dot_general(
        a, b, (((1,), (0,)), ((), ())), precision=lax.Precision.HIGHEST, preferred_element_type=F32
    )


def split(value):
    high = value.astype(BF16)
    return high, (value - high.astype(F32)).astype(BF16)


def rows_by(rows, parts, contract):
    count = rows.shape[0]
    high, low = split(rows)
    dims = (((1,), (contract,)), ((), ()))
    both = jnp.concatenate([high.astype(F32), low.astype(F32)], axis=0).astype(BF16)
    first = lax.dot_general(both, parts[0], dims, preferred_element_type=F32)
    total = first[:count] + first[count:]
    if len(parts) > 1:
        total = total + lax.dot_general(high, parts[1], dims, preferred_element_type=F32)
    return total


def rows_nn(rows, *parts):
    return rows_by(rows, parts, 0)


def rows_nt(rows, *parts):
    return rows_by(rows, parts, 1)


def leaf_forward_kernel(y_ref, tgt_ref, rhs_ref, inv_ref, upd_ref, anc_ref, fwd_ref, send_ref):
    rhs_count, width = fwd_ref.shape[1:]
    peers, tiles = send_ref.shape[0:2]
    for pair in range(tiles - 1):
        parts = []
        for k in range(2):
            leaf = 2 * pair + k
            forward = lax.dot_general(
                rhs_ref[leaf], inv_ref[leaf], (((0,), (1,)), ((), ())), preferred_element_type=F32
            ).astype(BF16)
            fwd_ref[leaf] = forward
            update = lax.dot_general(
                forward, upd_ref[leaf], (((1,), (1,)), ((), ())), preferred_element_type=F32
            )
            parts.append(update.reshape(peers, COLS, width))
        send_ref[:, pair] = jnp.concatenate(parts, axis=1).astype(BF16)
    rows = anc_ref[...].T
    high = rows.astype(BF16).astype(F32)
    layer = y_ref[0]
    mine = jnp.where(layer == 0, high, jnp.where(layer == 1, rows - high, jnp.zeros_like(rows)))
    leaf = lax.broadcasted_iota(jnp.int32, (COLS, width), 1) // COLS
    names = jnp.zeros((COLS, width), F32)
    for k in range(tgt_ref.shape[0]):
        names = jnp.where(leaf == k, tgt_ref[k].astype(F32), names)
    names = jnp.broadcast_to(names[None], (peers, COLS, width))
    send_ref[:, tiles - 1] = jnp.concatenate([mine.reshape(peers, COLS, width), names], axis=1).astype(BF16)


def own_pair_kernel(inv_ref, cpl_ref, out_ref):
    inverse = inv_ref[0]
    out_ref[0], out_ref[1] = split(dot_nn(inverse, cpl_ref[0]))
    out_ref[2] = inverse.astype(BF16)


def transfer_kernel(x_count, x_ref, c_ref, *refs):
    pairs = refs[: 2 * x_count]
    m_ref, pack_ref, unit_ref, top_ref = refs[-4:]
    count, _, width = m_ref.shape[0:3]
    x, core = x_ref[0], c_ref[0]
    for d in range(x_count):
        for other in range(2):
            place = 2 * lax.rem(x + d, x_count) + jnp.where(other == 0, core, 1 - core)
            m_ref[place] = pairs[other * x_count + d][...]
    half = count // 2
    runs = []
    for k in range(count):
        if k % half == 0:
            run = m_ref[k, 0].astype(F32) + m_ref[k, 1].astype(F32)
        else:
            high, low = split(runs[-1])
            run = jnp.dot(m_ref[k, 0], high, preferred_element_type=F32)
            run += jnp.dot(m_ref[k, 0], low, preferred_element_type=F32)
            run += jnp.dot(m_ref[k, 1], high, preferred_element_type=F32)
        runs.append(run * -STEP_SCALE)
    first = jnp.concatenate(
        [runs[k] * STEP_SCALE ** (count - 1 - k) for k in range(half)], axis=0
    )
    second = jnp.concatenate(
        [runs[k] * STEP_SCALE ** (count - 1 - k) for k in range(half, count)], axis=0
    )
    second = rows_nn(second, *split(runs[half - 1]))
    stack = jnp.concatenate([first, second], axis=0)
    top = jnp.maximum(jnp.max(jnp.abs(stack)), 1e-30)
    unit = stack * (1.0 / top)
    unit_ref[0], unit_ref[1] = split(unit)
    high, low = split(unit.T)
    gram = lax.dot_general(high, high, (((1,), (1,)), ((), ())), preferred_element_type=F32)
    cross = lax.dot_general(high, low, (((1,), (1,)), ((), ())), preferred_element_type=F32)
    pack_ref[0], pack_ref[1] = split(stack[width * (count - 1) :])
    pack_ref[2] = (gram + (cross + cross.T)).astype(BF16)
    top_ref[...] = jnp.full(top_ref.shape, top, F32)


def order_kernel(z_ref, *refs):
    out_ref = refs[-1]
    count = out_ref.shape[0]
    for d in range(count):
        out_ref[lax.rem(z_ref[0] // 2 + d, count)] = refs[d][...]


def densify_kernel(plane_size, z_ref, c_ref, v_ref, dense_ref, code_ref, acc_ref):
    sources, tiles, rows, width = v_ref.shape
    planes = dense_ref.shape[0]
    body = (tiles - 1) * rows
    lane = lax.broadcasted_iota(jnp.int32, (sources, body), 1)
    last = v_ref[:, tiles - 1].astype(F32)
    codes = last[:, COLS, :].astype(jnp.int32) * COLS + lane % COLS
    by_core = codes.astype(F32).reshape(sources // 2, 2, body)
    code_ref[...] = jnp.where(c_ref[0] == 0, by_core[:, 0], by_core[:, 1]).T
    row = lax.broadcasted_iota(jnp.int32, (acc_ref.shape[0], body), 0)
    total = None
    for s in range(0, sources, 2):
        pick = jnp.concatenate(
            [(row == codes[s + i : s + i + 1, :]).astype(F32).astype(BF16) for i in range(2)], axis=1
        )
        both = v_ref[s : s + 2, 0 : tiles - 1].reshape(2 * body, width)
        term = jnp.dot(pick, both, preferred_element_type=F32)
        total = term if total is None else total + term
    acc_ref[...] = -total
    own = pl.multiple_of(z_ref[0] * plane_size * COLS, plane_size * COLS)
    mine = last[0:plane_size, 0:COLS]
    for y in range(1, sources // plane_size):
        mine = mine + last[y * plane_size : (y + 1) * plane_size, 0:COLS]
    acc_ref[pl.ds(own, plane_size * COLS), :] += mine.reshape(plane_size * COLS, width)
    dense_ref[...] = acc_ref[...].astype(BF16).reshape(dense_ref.shape)


def block_solve_kernel(e_ref, m_ref, unit_ref, top_ref, b_ref, out_ref):
    count = m_ref.shape[0]
    reduced = e_ref[0].astype(F32)
    for s in range(1, e_ref.shape[0]):
        reduced = reduced + e_ref[s].astype(F32)
    solved = []
    for j in range(count):
        b = rows_nt(reduced[COLS * j : COLS * (j + 1)], m_ref[j, 2])
        b_ref[COLS * j : COLS * (j + 1), :] = b
        if j > 0:
            b = b - rows_nt(solved[-1], m_ref[j, 0], m_ref[j, 1])
        solved.append(b)
    half_grow = STEP_SCALE ** (-count // 2)
    back = rows_nn(jnp.concatenate(solved, axis=1), unit_ref[0], unit_ref[1])
    back = -((back * half_grow) * top_ref[...] * half_grow)
    ends = jnp.concatenate([solved[-1], back, top_ref[...]], axis=0)
    for z in range(out_ref.shape[0]):
        out_ref[z] = ends


def carry_kernel(z_ref, c_ref, ends_ref, mine_ref, other_ref, b_ref, m_ref, x_ref, pack_ref):
    planes = ends_ref.shape[0]
    count, _, width = m_ref.shape[0:3]
    core = c_ref[0]
    for i in range(planes // 2):
        pack_ref[2 * i + core] = mine_ref[i]
        pack_ref[2 * i + 1 - core] = other_ref[i]
    grow = STEP_SCALE**-count
    half_grow = STEP_SCALE ** (-count // 2)
    own = z_ref[0]
    state = jnp.zeros((COLS, width), F32)
    inflow = state
    backs = []
    for z in range(planes):
        leaving, back, top = (ends_ref[z, COLS * i : COLS * (i + 1)] for i in range(3))
        if z > 0:
            answer = rows_nn(state, pack_ref[z, 2])
            for _ in range(2):
                answer = (answer * half_grow) * top * half_grow
            back = back - answer
            leaving = leaving + grow * rows_nt(state, pack_ref[z, 0], pack_ref[z, 1])
        backs.append(back)
        state = leaving
        if z < planes - 1:
            inflow = jnp.where(own == z + 1, state, inflow)
    state = jnp.zeros((COLS, width), F32)
    running = state
    for z in reversed(range(1, planes)):
        leaving = backs[z]
        if z < planes - 1:
            leaving = leaving + grow * rows_nn(state, pack_ref[z, 0], pack_ref[z, 1])
        state = leaving
        running = jnp.where(own == z - 1, state, running)
    solved = []
    for j in range(count):
        inflow = b_ref[COLS * j : COLS * (j + 1), :] - rows_nt(inflow, m_ref[j, 0], m_ref[j, 1])
        solved.append(inflow)
    answers = [None] * count
    for j in reversed(range(count)):
        right = solved[j] - running
        if j > 0:
            running = rows_nn(right, m_ref[j, 0], m_ref[j, 1])
        answers[j] = rows_nn(right, m_ref[j, 2])
    coarse = jnp.concatenate(answers, axis=0).astype(BF16)
    for z in range(x_ref.shape[0]):
        x_ref[z] = coarse


def choose_kernel(plane_size, z_ref, c_ref, x_ref, other_ref, code_ref, send_ref):
    peers, tiles, rows, width = send_ref.shape
    planes = x_ref.shape[0]
    body = code_ref.shape[0]
    core = c_ref[0]
    lane = lax.broadcasted_iota(jnp.int32, (body, planes * plane_size * COLS), 1)
    codes = code_ref[...].astype(jnp.int32)
    x_count = plane_size // 2
    mine, theirs = x_ref[...].astype(F32), other_ref[...].astype(F32)
    halves = [jnp.where(core == half, mine, theirs).reshape(lane.shape[1], width) for half in range(2)]
    values = jnp.concatenate(halves, axis=1).astype(BF16)
    mine, theirs = x_ref[z_ref[0]].astype(F32), other_ref[z_ref[0]].astype(F32)
    own = [jnp.where(core == half, mine, theirs) for half in range(2)]
    for d in range(peers):
        pick = (lane == codes[:, d : d + 1]).astype(F32).astype(BF16)
        chosen = jnp.dot(pick, values, preferred_element_type=F32).astype(BF16)
        for half in range(2):
            part = chosen[:, width * half : width * (half + 1)].reshape(body // rows, rows, width)
            for pair in range(body // rows):
                send_ref[d, 2 * pair + half] = part[pair]
        j = 2 * (d % x_count)
        ends = [
            jnp.where(
                core == 0, own[half][COLS * j : COLS * (j + 1)], own[half][COLS * (j + 1) : COLS * (j + 2)]
            )
            for half in range(2)
        ]
        send_ref[d, tiles - 1] = jnp.concatenate(ends, axis=0).astype(BF16)


def leaf_backward_kernel(w_ref, tail_ref, fwd_ref, inv_ref, upd_ref, out_ref, anc_ref):
    step = pl.program_id(0)
    peers, _, rows, width = w_ref.shape
    rhs_count = fwd_ref.shape[1]
    for pair in range(LEAF_STEP // 2):
        came = [w_ref[:, 2 * pair + half].astype(F32) for half in range(2)]
        for k in range(2):
            leaf = 2 * pair + k
            both = jnp.concatenate([c[:, k * COLS : (k + 1) * COLS, :] for c in came], axis=1)
            chosen = both.reshape(rhs_count, width).astype(BF16)
            correction = jnp.dot(chosen, upd_ref[leaf], preferred_element_type=F32)
            residue = (fwd_ref[leaf].astype(F32) - correction).astype(BF16)
            out_ref[leaf] = lax.dot_general(
                inv_ref[leaf], residue, (((0,), (1,)), ((), ())), preferred_element_type=F32
            ).astype(BF16)

    @pl.when(step == 0)
    def _():
        anc_ref[...] = tail_ref[:, 0].astype(F32).reshape(rhs_count, width).T


SMEM = pl.BlockSpec(memory_space=pltpu.SMEM)


def call(kernel, operands, outs, scratch=(), flops=0, after=(), vmem=16):
    moved = sum(a.size * a.dtype.itemsize for a in list(operands) + list(outs))
    if after:
        inner, count = kernel, len(operands)
        kernel = lambda *refs: inner(*refs[:count], *refs[count + len(after) :])
    return pl.pallas_call(
        kernel,
        out_shape=outs,
        in_specs=[
            SMEM if a.dtype == jnp.int32 else pl.BlockSpec(memory_space=pltpu.VMEM) for a in operands
        ]
        + [pl.BlockSpec(memory_space=pl.ANY) for _ in after],
        out_specs=[pl.BlockSpec(memory_space=pltpu.VMEM) for _ in outs],
        scratch_shapes=list(scratch),
        compiler_params=pltpu.CompilerParams(vmem_limit_bytes=vmem * 2**20),
        cost_estimate=pl.CostEstimate(flops=flops, bytes_accessed=moved, transcendentals=0),
    )(*operands, *after)


def shift(value, axis, by):
    size = lax.axis_size(axis)
    return lax.ppermute(value, axis, [((i + by) % size, i) for i in range(size)])


def every_other(value, by):
    half = lax.axis_size("z") // 2
    return lax.ppermute(
        value,
        ("z", "c"),
        [
            (2 * (2 * ((z // 2 + by) % half) + c) + z % 2, 2 * z + c)
            for z in range(2 * half)
            for c in range(2)
        ],
    )


def local(leaf_rhs, leaf_inverse, leaf_update, leaf_target, anc_rhs, anc_inverse, anc_coupling):
    rhs, inv, upd = leaf_rhs[0], leaf_inverse[0], leaf_update[0]
    leaves, width, rhs_count = rhs.shape
    peers = lax.axis_size(PLANE_AXES)
    both_peers = 2 * peers
    planes = lax.axis_size("z")
    x_count = lax.axis_size("x")
    plane_size = 2 * x_count
    chain = planes * plane_size
    pairs = leaves // 2
    sds = jax.ShapeDtypeStruct
    y_index, z_index, x_index, c_index = (
        lax.axis_index(a).astype(jnp.int32).reshape(1) for a in ("y", "z", "x", "c")
    )

    (own_pair,) = call(own_pair_kernel, (anc_inverse, anc_coupling), [sds((3, width, width), BF16)], vmem=60)
    along = [own_pair] + [shift(own_pair, "x", d) for d in range(1, x_count)]

    whole = lambda shape: pl.BlockSpec(shape, lambda i: (0,) * len(shape))
    sent = (both_peers, pairs + 1, 2 * COLS, width)
    forward, send = pl.pallas_call(
        leaf_forward_kernel,
        grid=(1,),
        out_shape=[sds((leaves, rhs_count, width), BF16), sds(sent, BF16)],
        in_specs=[SMEM, SMEM] + [whole(a.shape) for a in (rhs, inv, upd, anc_rhs[0])],
        out_specs=[whole((leaves, rhs_count, width)), whole(sent)],
        compiler_params=pltpu.CompilerParams(
            dimension_semantics=("arbitrary",), vmem_limit_bytes=60 * 2**20
        ),
    )(y_index, leaf_target.astype(jnp.int32).reshape(leaves), rhs, inv, upd, anc_rhs[0])

    send, *along = lax.optimization_barrier((send, *along))
    came = lax.all_to_all(send.reshape(both_peers, -1, width), CORE_AXES, 0, 0, tiled=True).reshape(sent)

    across = [shift(pair, "c", 1) for pair in along]
    m_blocks, pack, unit, top = call(
        functools.partial(transfer_kernel, x_count),
        (x_index, c_index, *along, *across),
        [
            sds((plane_size, 3, width, width), BF16),
            sds((3, width, width), BF16),
            sds((2, plane_size * width, width), BF16),
            sds((COLS, width), F32),
        ],
    )
    packs = [every_other(pack, d) for d in range(planes // 2)]

    dense, codes = call(
        functools.partial(densify_kernel, plane_size),
        (z_index, c_index, came),
        [
            sds((planes, plane_size * COLS, width), BF16),
            sds((leaves * COLS, peers), F32),
        ],
        scratch=[pltpu.VMEM((chain * COLS, width), F32)],
    )
    dense, *packs = lax.optimization_barrier((dense, *packs))
    sums = lax.all_to_all(dense, "z", 0, 0, tiled=True)
    (own_packs,) = call(order_kernel, (z_index, *packs), [sds((planes // 2, 3, width, width), BF16)])
    other_packs = shift(own_packs, "c", 1)
    b_rows, ends = call(
        block_solve_kernel,
        (sums, m_blocks, unit, top),
        [sds((plane_size * COLS, width), F32), sds((planes, 3 * COLS, width), F32)],
    )
    all_ends = lax.all_to_all(ends, "z", 0, 0, tiled=True)
    (x_rows,) = call(
        carry_kernel,
        (z_index, c_index, all_ends, own_packs, other_packs, b_rows, m_blocks),
        [sds((planes, plane_size * COLS, width), BF16)],
        scratch=[pltpu.VMEM((planes, 3, width, width), BF16)],
    )
    all_x = lax.all_to_all(x_rows, "z", 0, 0, tiled=True)
    other_x = shift(all_x, "c", 1)
    (answer,) = call(
        functools.partial(choose_kernel, plane_size),
        (z_index, c_index, all_x, other_x, codes),
        [sds((peers, 2 * pairs + 1, 2 * COLS, width), BF16)],
    )
    answers = lax.all_to_all(answer.reshape(peers, -1, width), PLANE_AXES, 0, 0, tiled=True)
    answers = answers.reshape(answer.shape)

    leaf = lambda i: (i, 0, 0)
    leaf_solution, anc_solution = pl.pallas_call(
        leaf_backward_kernel,
        grid=(leaves // LEAF_STEP,),
        out_shape=[sds((leaves, width, rhs_count), BF16), sds((width, rhs_count), F32)],
        in_specs=[
            pl.BlockSpec((peers, LEAF_STEP, 2 * COLS, width), lambda i: (0, i, 0, 0)),
            pl.BlockSpec((peers, 1, 2 * COLS, width), lambda i: (0, 2 * pairs, 0, 0)),
            pl.BlockSpec((LEAF_STEP, rhs_count, width), leaf),
            pl.BlockSpec((LEAF_STEP, width, width), leaf),
            pl.BlockSpec((LEAF_STEP, width, width), leaf),
        ],
        out_specs=[
            pl.BlockSpec((LEAF_STEP, width, rhs_count), leaf),
            pl.BlockSpec((width, rhs_count), lambda i: (0, 0)),
        ],
        compiler_params=pltpu.CompilerParams(
            dimension_semantics=("arbitrary",), vmem_limit_bytes=40 * 2**20
        ),
    )(answers, answers, forward, inv, upd)
    return (leaf_solution[None], anc_solution[None])


def build(mesh, sizes):
    inner = Mesh(mesh.devices.reshape(sizes), ("y", "z", "x", "c"))
    leaf4 = P("y", ("z", "x", "c"), None, None)
    owner = P(("z", "x", "c"), None, None)
    return jax.shard_map(
        local,
        mesh=inner,
        in_specs=(leaf4, leaf4, leaf4, P("y", ("z", "x", "c"), None), owner, owner, owner),
        out_specs=(leaf4, owner),
        check_vma=False,
    )


def solution(mesh):
    return build(mesh, (4, 8, 4, 2))
```

```python
import functools

import jax
import jax.numpy as jnp
from jax import lax
from jax.experimental import pallas as pl
from jax.experimental.pallas import tpu as pltpu
from jax.sharding import Mesh
from jax.sharding import PartitionSpec as P

F32 = jnp.float32
BF16 = jnp.bfloat16
PLANE_AXES = ("y", "x")
CORE_AXES = ("y", "x", "c")
STEP_SCALE = 2.0**-8
COLS = 8
LEAF_STEP = 8


def dot_nn(a, b):
    return lax.dot_general(
        a, b, (((1,), (0,)), ((), ())), precision=lax.Precision.HIGHEST, preferred_element_type=F32
    )


def split(value):
    high = value.astype(BF16)
    return high, (value - high.astype(F32)).astype(BF16)


def rows_by(rows, parts, contract):
    count = rows.shape[0]
    high, low = split(rows)
    dims = (((1,), (contract,)), ((), ()))
    both = jnp.concatenate([high.astype(F32), low.astype(F32)], axis=0).astype(BF16)
    first = lax.dot_general(both, parts[0], dims, preferred_element_type=F32)
    total = first[:count] + first[count:]
    if len(parts) > 1:
        total = total + lax.dot_general(high, parts[1], dims, preferred_element_type=F32)
    return total


def rows_nn(rows, *parts):
    return rows_by(rows, parts, 0)


def rows_nt(rows, *parts):
    return rows_by(rows, parts, 1)


def leaf_forward_kernel(y_ref, tgt_ref, rhs_ref, inv_ref, upd_ref, anc_ref, fwd_ref, send_ref):
    rhs_count, width = fwd_ref.shape[1:]
    peers, tiles = send_ref.shape[0:2]
    for pair in range(tiles - 1):
        parts = []
        for k in range(2):
            leaf = 2 * pair + k
            forward = lax.dot_general(
                rhs_ref[leaf], inv_ref[leaf], (((0,), (1,)), ((), ())), preferred_element_type=F32
            ).astype(BF16)
            fwd_ref[leaf] = forward
            update = lax.dot_general(
                forward, upd_ref[leaf], (((1,), (1,)), ((), ())), preferred_element_type=F32
            )
            parts.append(update.reshape(peers, COLS, width))
        send_ref[:, pair] = jnp.concatenate(parts, axis=1).astype(BF16)
    rows = anc_ref[...].T
    high = rows.astype(BF16).astype(F32)
    layer = y_ref[0]
    mine = jnp.where(layer == 0, high, jnp.where(layer == 1, rows - high, jnp.zeros_like(rows)))
    leaf = lax.broadcasted_iota(jnp.int32, (COLS, width), 1) // COLS
    names = jnp.zeros((COLS, width), F32)
    for k in range(tgt_ref.shape[0]):
        names = jnp.where(leaf == k, tgt_ref[k].astype(F32), names)
    names = jnp.broadcast_to(names[None], (peers, COLS, width))
    send_ref[:, tiles - 1] = jnp.concatenate([mine.reshape(peers, COLS, width), names], axis=1).astype(BF16)


def own_pair_kernel(inv_ref, cpl_ref, out_ref):
    inverse = inv_ref[0]
    out_ref[0], out_ref[1] = split(dot_nn(inverse, cpl_ref[0]))
    out_ref[2] = inverse.astype(BF16)


def transfer_kernel(x_count, x_ref, c_ref, *refs):
    pairs = refs[: 2 * x_count]
    m_ref, pack_ref, unit_ref, top_ref = refs[-4:]
    count, _, width = m_ref.shape[0:3]
    x, core = x_ref[0], c_ref[0]
    for d in range(x_count):
        for other in range(2):
            place = 2 * lax.rem(x + d, x_count) + jnp.where(other == 0, core, 1 - core)
            m_ref[place] = pairs[other * x_count + d][...]
    half = count // 2
    runs = []
    for k in range(count):
        if k % half == 0:
            run = m_ref[k, 0].astype(F32) + m_ref[k, 1].astype(F32)
        else:
            high, low = split(runs[-1])
            run = jnp.dot(m_ref[k, 0], high, preferred_element_type=F32)
            run += jnp.dot(m_ref[k, 0], low, preferred_element_type=F32)
            run += jnp.dot(m_ref[k, 1], high, preferred_element_type=F32)
        runs.append(run * -STEP_SCALE)
    first = jnp.concatenate(
        [runs[k] * STEP_SCALE ** (count - 1 - k) for k in range(half)], axis=0
    )
    second = jnp.concatenate(
        [runs[k] * STEP_SCALE ** (count - 1 - k) for k in range(half, count)], axis=0
    )
    second = rows_nn(second, *split(runs[half - 1]))
    stack = jnp.concatenate([first, second], axis=0)
    top = jnp.maximum(jnp.max(jnp.abs(stack)), 1e-30)
    unit = stack * (1.0 / top)
    unit_ref[0], unit_ref[1] = split(unit)
    high, low = split(unit.T)
    gram = lax.dot_general(high, high, (((1,), (1,)), ((), ())), preferred_element_type=F32)
    cross = lax.dot_general(high, low, (((1,), (1,)), ((), ())), preferred_element_type=F32)
    pack_ref[0], pack_ref[1] = split(stack[width * (count - 1) :])
    pack_ref[2] = (gram + (cross + cross.T)).astype(BF16)
    top_ref[...] = jnp.full(top_ref.shape, top, F32)


def late_kernel(m_ref, late_ref, top_ref):
    count = m_ref.shape[0]
    half = count // 2
    runs = [None] * count
    for k in reversed(range(count)):
        if k % half == half - 1:
            run = m_ref[k, 0].astype(F32) + m_ref[k, 1].astype(F32)
        else:
            run = rows_nn(runs[k + 1], m_ref[k, 0], m_ref[k, 1])
        runs[k] = run * -STEP_SCALE
    shared = runs[half]
    first = rows_nn(shared, *split(jnp.concatenate(runs[:half], axis=1)))
    width = shared.shape[0]
    pieces = [first[:, width * k : width * (k + 1)] for k in range(half)] + runs[half:]
    stack = jnp.concatenate([pieces[k] * STEP_SCALE**k for k in range(count)], axis=1)
    top = jnp.maximum(jnp.max(jnp.abs(stack)), 1e-30)
    late_ref[0], late_ref[1] = split(stack * (1.0 / top))
    top_ref[...] = jnp.full(top_ref.shape, top, F32)


def order_kernel(z_ref, *refs):
    out_ref = refs[-1]
    count = out_ref.shape[0]
    for d in range(count):
        out_ref[lax.rem(z_ref[0] // 2 + d, count)] = refs[d][...]


def densify_kernel(plane_size, z_ref, c_ref, v_ref, dense_ref, code_ref, acc_ref):
    sources, tiles, rows, width = v_ref.shape
    planes = dense_ref.shape[0]
    body = (tiles - 1) * rows
    lane = lax.broadcasted_iota(jnp.int32, (sources, body), 1)
    last = v_ref[:, tiles - 1].astype(F32)
    codes = last[:, COLS, :].astype(jnp.int32) * COLS + lane % COLS
    by_core = codes.astype(F32).reshape(sources // 2, 2, body)
    code_ref[...] = jnp.where(c_ref[0] == 0, by_core[:, 0], by_core[:, 1]).T
    row = lax.broadcasted_iota(jnp.int32, (acc_ref.shape[0], body), 0)
    total = None
    for s in range(0, sources, 2):
        pick = jnp.concatenate(
            [(row == codes[s + i : s + i + 1, :]).astype(F32).astype(BF16) for i in range(2)], axis=1
        )
        both = v_ref[s : s + 2, 0 : tiles - 1].reshape(2 * body, width)
        term = jnp.dot(pick, both, preferred_element_type=F32)
        total = term if total is None else total + term
    acc_ref[...] = -total
    own = pl.multiple_of(z_ref[0] * plane_size * COLS, plane_size * COLS)
    mine = last[0:plane_size, 0:COLS]
    for y in range(1, sources // plane_size):
        mine = mine + last[y * plane_size : (y + 1) * plane_size, 0:COLS]
    acc_ref[pl.ds(own, plane_size * COLS), :] += mine.reshape(plane_size * COLS, width)
    dense_ref[...] = acc_ref[...].astype(BF16).reshape(dense_ref.shape)


def block_solve_kernel(e_ref, m_ref, unit_ref, top_ref, s_ref, out_ref):
    count = m_ref.shape[0]
    reduced = e_ref[0].astype(F32)
    for s in range(1, e_ref.shape[0]):
        reduced = reduced + e_ref[s].astype(F32)
    solved = []
    for j in range(count):
        b = rows_nt(reduced[COLS * j : COLS * (j + 1)], m_ref[j, 2])
        if j > 0:
            b = b - rows_nt(solved[-1], m_ref[j, 0], m_ref[j, 1])
        solved.append(b)
    half_grow = STEP_SCALE ** (-count // 2)
    solved_wide = jnp.concatenate(solved, axis=1)
    s_ref[...] = solved_wide
    back = rows_nn(solved_wide, unit_ref[0], unit_ref[1])
    back = -((back * half_grow) * top_ref[...] * half_grow)
    ends = jnp.concatenate([solved[-1], back, top_ref[...]], axis=0)
    for z in range(out_ref.shape[0]):
        out_ref[z] = ends


def carry_kernel(
    z_ref, c_ref, ends_ref, mine_ref, other_ref, s_ref, m_ref, unit_ref, top_ref, late_ref, late_top_ref, x_ref, pack_ref
):
    planes = ends_ref.shape[0]
    count, _, width = m_ref.shape[0:3]
    core = c_ref[0]
    for i in range(planes // 2):
        pack_ref[2 * i + core] = mine_ref[i]
        pack_ref[2 * i + 1 - core] = other_ref[i]
    grow = STEP_SCALE**-count
    half_grow = STEP_SCALE ** (-count // 2)
    own = z_ref[0]
    state = jnp.zeros((COLS, width), F32)
    inflow = state
    backs = []
    for z in range(planes):
        leaving, back, top = (ends_ref[z, COLS * i : COLS * (i + 1)] for i in range(3))
        if z > 0:
            answer = rows_nn(state, pack_ref[z, 2])
            for _ in range(2):
                answer = (answer * half_grow) * top * half_grow
            back = back - answer
            leaving = leaving + grow * rows_nt(state, pack_ref[z, 0], pack_ref[z, 1])
        backs.append(back)
        state = leaving
        if z < planes - 1:
            inflow = jnp.where(own == z + 1, state, inflow)
    gain = rows_nt(inflow, unit_ref[0], unit_ref[1])
    solved = s_ref[...] + (gain * half_grow) * top_ref[:, 0:1] * half_grow
    solved = [solved[:, width * k : width * (k + 1)] for k in range(count)]
    state = jnp.zeros((COLS, width), F32)
    running = state
    after = [None] * (count + 1)
    for i in range(max(planes, count) - 1):
        z, j = planes - 1 - i, count - 1 - i
        if z > 0:
            leaving = backs[z]
            if z < planes - 1:
                leaving = leaving + grow * rows_nn(state, pack_ref[z, 0], pack_ref[z, 1])
            state = leaving
            running = jnp.where(own == z - 1, state, running)
        if j > 0:
            right = solved[j] if after[j + 1] is None else solved[j] - after[j + 1]
            after[j] = rows_nn(right, m_ref[j, 0], m_ref[j, 1])
    gain = rows_nn(running, late_ref[0], late_ref[1])
    gain = (gain * half_grow) * late_top_ref[:, 0:1] * half_grow
    answers = []
    for j in range(count):
        if j < count - 1:
            right = solved[j] - (after[j + 1] + gain[:, width * (j + 1) : width * (j + 2)])
        else:
            right = solved[j] - running
        answers.append(rows_nn(right, m_ref[j, 2]))
    coarse = jnp.concatenate(answers, axis=0).astype(BF16)
    for z in range(x_ref.shape[0]):
        x_ref[z] = coarse


def choose_kernel(plane_size, z_ref, c_ref, x_ref, other_ref, code_ref, send_ref):
    peers, tiles, rows, width = send_ref.shape
    planes = x_ref.shape[0]
    body = code_ref.shape[0]
    core = c_ref[0]
    lane = lax.broadcasted_iota(jnp.int32, (body, planes * plane_size * COLS), 1)
    codes = code_ref[...].astype(jnp.int32)
    x_count = plane_size // 2
    mine, theirs = x_ref[...].astype(F32), other_ref[...].astype(F32)
    halves = [jnp.where(core == half, mine, theirs).reshape(lane.shape[1], width) for half in range(2)]
    values = jnp.concatenate(halves, axis=1).astype(BF16)
    mine, theirs = x_ref[z_ref[0]].astype(F32), other_ref[z_ref[0]].astype(F32)
    own = [jnp.where(core == half, mine, theirs) for half in range(2)]
    for d in range(peers):
        pick = (lane == codes[:, d : d + 1]).astype(F32).astype(BF16)
        chosen = jnp.dot(pick, values, preferred_element_type=F32).astype(BF16)
        for half in range(2):
            part = chosen[:, width * half : width * (half + 1)].reshape(body // rows, rows, width)
            for pair in range(body // rows):
                send_ref[d, 2 * pair + half] = part[pair]
        j = 2 * (d % x_count)
        ends = [
            jnp.where(
                core == 0, own[half][COLS * j : COLS * (j + 1)], own[half][COLS * (j + 1) : COLS * (j + 2)]
            )
            for half in range(2)
        ]
        send_ref[d, tiles - 1] = jnp.concatenate(ends, axis=0).astype(BF16)


def leaf_backward_kernel(w_ref, tail_ref, fwd_ref, inv_ref, upd_ref, out_ref, anc_ref):
    step = pl.program_id(0)
    peers, _, rows, width = w_ref.shape
    rhs_count = fwd_ref.shape[1]
    for pair in range(LEAF_STEP // 2):
        came = [w_ref[:, 2 * pair + half].astype(F32) for half in range(2)]
        for k in range(2):
            leaf = 2 * pair + k
            both = jnp.concatenate([c[:, k * COLS : (k + 1) * COLS, :] for c in came], axis=1)
            chosen = both.reshape(rhs_count, width).astype(BF16)
            correction = jnp.dot(chosen, upd_ref[leaf], preferred_element_type=F32)
            residue = (fwd_ref[leaf].astype(F32) - correction).astype(BF16)
            out_ref[leaf] = lax.dot_general(
                inv_ref[leaf], residue, (((0,), (1,)), ((), ())), preferred_element_type=F32
            ).astype(BF16)

    @pl.when(step == 0)
    def _():
        anc_ref[...] = tail_ref[:, 0].astype(F32).reshape(rhs_count, width).T


SMEM = pl.BlockSpec(memory_space=pltpu.SMEM)


def call(kernel, operands, outs, scratch=(), flops=0, after=(), vmem=16):
    moved = sum(a.size * a.dtype.itemsize for a in list(operands) + list(outs))
    if after:
        inner, count = kernel, len(operands)
        kernel = lambda *refs: inner(*refs[:count], *refs[count + len(after) :])
    return pl.pallas_call(
        kernel,
        out_shape=outs,
        in_specs=[
            SMEM if a.dtype == jnp.int32 else pl.BlockSpec(memory_space=pltpu.VMEM) for a in operands
        ]
        + [pl.BlockSpec(memory_space=pl.ANY) for _ in after],
        out_specs=[pl.BlockSpec(memory_space=pltpu.VMEM) for _ in outs],
        scratch_shapes=list(scratch),
        compiler_params=pltpu.CompilerParams(vmem_limit_bytes=vmem * 2**20),
        cost_estimate=pl.CostEstimate(flops=flops, bytes_accessed=moved, transcendentals=0),
    )(*operands, *after)


def shift(value, axis, by):
    size = lax.axis_size(axis)
    return lax.ppermute(value, axis, [((i + by) % size, i) for i in range(size)])


def every_other(value, by):
    half = lax.axis_size("z") // 2
    return lax.ppermute(
        value,
        ("z", "c"),
        [
            (2 * (2 * ((z // 2 + by) % half) + c) + z % 2, 2 * z + c)
            for z in range(2 * half)
            for c in range(2)
        ],
    )


def local(leaf_rhs, leaf_inverse, leaf_update, leaf_target, anc_rhs, anc_inverse, anc_coupling):
    rhs, inv, upd = leaf_rhs[0], leaf_inverse[0], leaf_update[0]
    leaves, width, rhs_count = rhs.shape
    peers = lax.axis_size(PLANE_AXES)
    both_peers = 2 * peers
    planes = lax.axis_size("z")
    x_count = lax.axis_size("x")
    plane_size = 2 * x_count
    chain = planes * plane_size
    pairs = leaves // 2
    sds = jax.ShapeDtypeStruct
    y_index, z_index, x_index, c_index = (
        lax.axis_index(a).astype(jnp.int32).reshape(1) for a in ("y", "z", "x", "c")
    )

    (own_pair,) = call(own_pair_kernel, (anc_inverse, anc_coupling), [sds((3, width, width), BF16)], vmem=60)
    along = [own_pair] + [shift(own_pair, "x", d) for d in range(1, x_count)]

    whole = lambda shape: pl.BlockSpec(shape, lambda i: (0,) * len(shape))
    sent = (both_peers, pairs + 1, 2 * COLS, width)
    forward, send = pl.pallas_call(
        leaf_forward_kernel,
        grid=(1,),
        out_shape=[sds((leaves, rhs_count, width), BF16), sds(sent, BF16)],
        in_specs=[SMEM, SMEM] + [whole(a.shape) for a in (rhs, inv, upd, anc_rhs[0])],
        out_specs=[whole((leaves, rhs_count, width)), whole(sent)],
        compiler_params=pltpu.CompilerParams(
            dimension_semantics=("arbitrary",), vmem_limit_bytes=60 * 2**20
        ),
    )(y_index, leaf_target.astype(jnp.int32).reshape(leaves), rhs, inv, upd, anc_rhs[0])

    send, *along = lax.optimization_barrier((send, *along))
    came = lax.all_to_all(send.reshape(both_peers, -1, width), CORE_AXES, 0, 0, tiled=True).reshape(sent)

    across = [shift(pair, "c", 1) for pair in along]
    m_blocks, pack, unit, top = call(
        functools.partial(transfer_kernel, x_count),
        (x_index, c_index, *along, *across),
        [
            sds((plane_size, 3, width, width), BF16),
            sds((3, width, width), BF16),
            sds((2, plane_size * width, width), BF16),
            sds((COLS, width), F32),
        ],
    )
    packs = [every_other(pack, d) for d in range(planes // 2)]

    dense, codes = call(
        functools.partial(densify_kernel, plane_size),
        (z_index, c_index, came),
        [
            sds((planes, plane_size * COLS, width), BF16),
            sds((leaves * COLS, peers), F32),
        ],
        scratch=[pltpu.VMEM((chain * COLS, width), F32)],
    )
    dense, *packs = lax.optimization_barrier((dense, *packs))
    sums = lax.all_to_all(dense, "z", 0, 0, tiled=True)
    (own_packs,) = call(order_kernel, (z_index, *packs), [sds((planes // 2, 3, width, width), BF16)])
    other_packs = shift(own_packs, "c", 1)
    late, late_top = call(
        late_kernel,
        (m_blocks,),
        [sds((2, width, plane_size * width), BF16), sds((COLS, width), F32)],
    )
    s_wide, ends = call(
        block_solve_kernel,
        (sums, m_blocks, unit, top),
        [sds((COLS, plane_size * width), F32), sds((planes, 3 * COLS, width), F32)],
    )
    ends, other_packs, late, late_top = lax.optimization_barrier((ends, other_packs, late, late_top))
    all_ends = lax.all_to_all(ends, "z", 0, 0, tiled=True)
    (x_rows,) = call(
        carry_kernel,
        (z_index, c_index, all_ends, own_packs, other_packs, s_wide, m_blocks, unit, top, late, late_top),
        [sds((planes, plane_size * COLS, width), BF16)],
        scratch=[pltpu.VMEM((planes, 3, width, width), BF16)],
    )
    all_x = lax.all_to_all(x_rows, "z", 0, 0, tiled=True)
    other_x = shift(all_x, "c", 1)
    (answer,) = call(
        functools.partial(choose_kernel, plane_size),
        (z_index, c_index, all_x, other_x, codes),
        [sds((peers, 2 * pairs + 1, 2 * COLS, width), BF16)],
    )
    answers = lax.all_to_all(answer.reshape(peers, -1, width), PLANE_AXES, 0, 0, tiled=True)
    answers = answers.reshape(answer.shape)

    leaf = lambda i: (i, 0, 0)
    leaf_solution, anc_solution = pl.pallas_call(
        leaf_backward_kernel,
        grid=(leaves // LEAF_STEP,),
        out_shape=[sds((leaves, width, rhs_count), BF16), sds((width, rhs_count), F32)],
        in_specs=[
            pl.BlockSpec((peers, LEAF_STEP, 2 * COLS, width), lambda i: (0, i, 0, 0)),
            pl.BlockSpec((peers, 1, 2 * COLS, width), lambda i: (0, 2 * pairs, 0, 0)),
            pl.BlockSpec((LEAF_STEP, rhs_count, width), leaf),
            pl.BlockSpec((LEAF_STEP, width, width), leaf),
            pl.BlockSpec((LEAF_STEP, width, width), leaf),
        ],
        out_specs=[
            pl.BlockSpec((LEAF_STEP, width, rhs_count), leaf),
            pl.BlockSpec((width, rhs_count), lambda i: (0, 0)),
        ],
        compiler_params=pltpu.CompilerParams(
            dimension_semantics=("arbitrary",), vmem_limit_bytes=40 * 2**20
        ),
    )(answers, answers, forward, inv, upd)
    return (leaf_solution[None], anc_solution[None])


def build(mesh, sizes):
    inner = Mesh(mesh.devices.reshape(sizes), ("y", "z", "x", "c"))
    leaf4 = P("y", ("z", "x", "c"), None, None)
    owner = P(("z", "x", "c"), None, None)
    return jax.shard_map(
        local,
        mesh=inner,
        in_specs=(leaf4, leaf4, leaf4, P("y", ("z", "x", "c"), None), owner, owner, owner),
        out_specs=(leaf4, owner),
        check_vma=False,
    )


def solution(mesh):
    return build(mesh, (4, 8, 4, 2))
```

```python
import functools

import jax
import jax.numpy as jnp
from jax import lax
from jax.experimental import pallas as pl
from jax.experimental.pallas import tpu as pltpu
from jax.sharding import Mesh
from jax.sharding import PartitionSpec as P

F32 = jnp.float32
BF16 = jnp.bfloat16
PLANE_AXES = ("y", "x")
CORE_AXES = ("y", "x", "c")
STEP_SCALE = 2.0**-8
COLS = 8
LEAF_STEP = 16


def dot_nn(a, b):
    return lax.dot_general(
        a, b, (((1,), (0,)), ((), ())), precision=lax.Precision.HIGHEST, preferred_element_type=F32
    )


def split(value):
    high = value.astype(BF16)
    return high, (value - high.astype(F32)).astype(BF16)


def rows_by(rows, parts, contract):
    count = rows.shape[0]
    high, low = split(rows)
    dims = (((1,), (contract,)), ((), ()))
    both = jnp.concatenate([high.astype(F32), low.astype(F32)], axis=0).astype(BF16)
    first = lax.dot_general(both, parts[0], dims, preferred_element_type=F32)
    total = first[:count] + first[count:]
    if len(parts) > 1:
        total = total + lax.dot_general(high, parts[1], dims, preferred_element_type=F32)
    return total


def rows_nn(rows, *parts):
    return rows_by(rows, parts, 0)


def rows_nt(rows, *parts):
    return rows_by(rows, parts, 1)


def leaf_forward_kernel(y_ref, tgt_ref, rhs_ref, inv_ref, upd_ref, anc_ref, fwd_ref, send_ref):
    rhs_count, width = fwd_ref.shape[1:]
    peers, tiles = send_ref.shape[0:2]
    for pair in range(tiles - 1):
        parts = []
        for k in range(2):
            leaf = 2 * pair + k
            forward = lax.dot_general(
                rhs_ref[leaf], inv_ref[leaf], (((0,), (1,)), ((), ())), preferred_element_type=F32
            ).astype(BF16)
            fwd_ref[leaf] = forward
            update = lax.dot_general(
                forward, upd_ref[leaf], (((1,), (1,)), ((), ())), preferred_element_type=F32
            )
            parts.append(update.reshape(peers, COLS, width))
        send_ref[:, pair] = jnp.concatenate(parts, axis=1).astype(BF16)
    rows = anc_ref[...].T
    high = rows.astype(BF16).astype(F32)
    layer = y_ref[0]
    mine = jnp.where(layer == 0, high, jnp.where(layer == 1, rows - high, jnp.zeros_like(rows)))
    leaf = lax.broadcasted_iota(jnp.int32, (COLS, width), 1) // COLS
    names = jnp.zeros((COLS, width), F32)
    for k in range(tgt_ref.shape[0]):
        names = jnp.where(leaf == k, tgt_ref[k].astype(F32), names)
    names = jnp.broadcast_to(names[None], (peers, COLS, width))
    send_ref[:, tiles - 1] = jnp.concatenate([mine.reshape(peers, COLS, width), names], axis=1).astype(BF16)


def own_pair_kernel(inv_ref, cpl_ref, out_ref):
    inverse = inv_ref[0]
    out_ref[0], out_ref[1] = split(dot_nn(inverse, cpl_ref[0]))
    out_ref[2] = inverse.astype(BF16)


def transfer_kernel(x_count, x_ref, c_ref, *refs):
    pairs = refs[: 2 * x_count]
    m_ref, pack_ref, unit_ref, top_ref = refs[-4:]
    count, _, width = m_ref.shape[0:3]
    x, core = x_ref[0], c_ref[0]
    for d in range(x_count):
        for other in range(2):
            place = 2 * lax.rem(x + d, x_count) + jnp.where(other == 0, core, 1 - core)
            m_ref[place] = pairs[other * x_count + d][...]
    half = count // 2
    runs = []
    for k in range(count):
        if k % half == 0:
            run = m_ref[k, 0].astype(F32) + m_ref[k, 1].astype(F32)
        else:
            high, low = split(runs[-1])
            run = jnp.dot(m_ref[k, 0], high, preferred_element_type=F32)
            run += jnp.dot(m_ref[k, 0], low, preferred_element_type=F32)
            run += jnp.dot(m_ref[k, 1], high, preferred_element_type=F32)
        runs.append(run * -STEP_SCALE)
    first = jnp.concatenate(
        [runs[k] * STEP_SCALE ** (count - 1 - k) for k in range(half)], axis=0
    )
    second = jnp.concatenate(
        [runs[k] * STEP_SCALE ** (count - 1 - k) for k in range(half, count)], axis=0
    )
    second = rows_nn(second, *split(runs[half - 1]))
    stack = jnp.concatenate([first, second], axis=0)
    top = jnp.maximum(jnp.max(jnp.abs(stack)), 1e-30)
    unit = stack * (1.0 / top)
    unit_ref[0], unit_ref[1] = split(unit)
    high, low = split(unit.T)
    gram = lax.dot_general(high, high, (((1,), (1,)), ((), ())), preferred_element_type=F32)
    cross = lax.dot_general(high, low, (((1,), (1,)), ((), ())), preferred_element_type=F32)
    pack_ref[0], pack_ref[1] = split(stack[width * (count - 1) :])
    pack_ref[2] = (gram + (cross + cross.T)).astype(BF16)
    top_ref[...] = jnp.full(top_ref.shape, top, F32)


def late_kernel(m_ref, late_ref, top_ref):
    count = m_ref.shape[0]
    half = count // 2
    runs = [None] * count
    for k in reversed(range(count)):
        if k % half == half - 1:
            run = m_ref[k, 0].astype(F32) + m_ref[k, 1].astype(F32)
        else:
            run = rows_nn(runs[k + 1], m_ref[k, 0], m_ref[k, 1])
        runs[k] = run * -STEP_SCALE
    shared = runs[half]
    first = rows_nn(shared, *split(jnp.concatenate(runs[:half], axis=1)))
    width = shared.shape[0]
    pieces = [first[:, width * k : width * (k + 1)] for k in range(half)] + runs[half:]
    stack = jnp.concatenate([pieces[k] * STEP_SCALE**k for k in range(count)], axis=1)
    top = jnp.maximum(jnp.max(jnp.abs(stack)), 1e-30)
    late_ref[0], late_ref[1] = split(stack * (1.0 / top))
    top_ref[...] = jnp.full(top_ref.shape, top, F32)


def order_kernel(steps, z_ref, *refs):
    out_ref = refs[-1]
    count = out_ref.shape[0]
    for i, d in enumerate(steps):
        out_ref[lax.rem(z_ref[0] // 2 + d, count)] = refs[i][...]


def densify_kernel(plane_size, z_ref, c_ref, v_ref, dense_ref, code_ref, acc_ref):
    sources, tiles, rows, width = v_ref.shape
    planes = dense_ref.shape[0]
    body = (tiles - 1) * rows
    lane = lax.broadcasted_iota(jnp.int32, (sources, body), 1)
    last = v_ref[:, tiles - 1].astype(F32)
    codes = last[:, COLS, :].astype(jnp.int32) * COLS + lane % COLS
    by_core = codes.astype(F32).reshape(sources // 2, 2, body)
    code_ref[...] = jnp.where(c_ref[0] == 0, by_core[:, 0], by_core[:, 1]).T
    row = lax.broadcasted_iota(jnp.int32, (acc_ref.shape[0], body), 0)
    total = None
    for s in range(0, sources, 2):
        pick = jnp.concatenate(
            [(row == codes[s + i : s + i + 1, :]).astype(F32).astype(BF16) for i in range(2)], axis=1
        )
        both = v_ref[s : s + 2, 0 : tiles - 1].reshape(2 * body, width)
        term = jnp.dot(pick, both, preferred_element_type=F32)
        total = term if total is None else total + term
    acc_ref[...] = -total
    own = pl.multiple_of(z_ref[0] * plane_size * COLS, plane_size * COLS)
    mine = last[0:plane_size, 0:COLS]
    for y in range(1, sources // plane_size):
        mine = mine + last[y * plane_size : (y + 1) * plane_size, 0:COLS]
    acc_ref[pl.ds(own, plane_size * COLS), :] += mine.reshape(plane_size * COLS, width)
    dense_ref[...] = acc_ref[...].astype(BF16).reshape(dense_ref.shape)


def block_solve_kernel(e_ref, m_ref, unit_ref, top_ref, s_ref, out_ref):
    count = m_ref.shape[0]
    reduced = e_ref[0].astype(F32)
    for s in range(1, e_ref.shape[0]):
        reduced = reduced + e_ref[s].astype(F32)
    solved = []
    for j in range(count):
        b = rows_nt(reduced[COLS * j : COLS * (j + 1)], m_ref[j, 2])
        if j > 0:
            b = b - rows_nt(solved[-1], m_ref[j, 0], m_ref[j, 1])
        solved.append(b)
    half_grow = STEP_SCALE ** (-count // 2)
    solved_wide = jnp.concatenate(solved, axis=1)
    s_ref[...] = solved_wide
    back = rows_nn(solved_wide, unit_ref[0], unit_ref[1])
    back = -((back * half_grow) * top_ref[...] * half_grow)
    ends = jnp.concatenate([solved[-1], back, top_ref[...]], axis=0)
    for z in range(out_ref.shape[0]):
        out_ref[z] = ends


def carry_kernel(
    z_ref, c_ref, ends_ref, mine_ref, other_ref, s_ref, m_ref, unit_ref, top_ref, late_ref, late_top_ref, x_ref, pack_ref
):
    planes = ends_ref.shape[0]
    count, _, width = m_ref.shape[0:3]
    core = c_ref[0]
    for i in range(planes // 2):
        pack_ref[2 * i + core] = mine_ref[i]
        pack_ref[2 * i + 1 - core] = other_ref[i]
    grow = STEP_SCALE**-count
    half_grow = STEP_SCALE ** (-count // 2)
    own = z_ref[0]
    state = jnp.zeros((COLS, width), F32)
    inflow = state
    backs = []
    for z in range(planes):
        leaving, back, top = (ends_ref[z, COLS * i : COLS * (i + 1)] for i in range(3))
        if z > 0:
            answer = rows_nn(state, pack_ref[z, 2])
            for _ in range(2):
                answer = (answer * half_grow) * top * half_grow
            back = back - answer
            leaving = leaving + grow * rows_nt(state, pack_ref[z, 0], pack_ref[z, 1])
        backs.append(back)
        state = leaving
        if z < planes - 1:
            inflow = jnp.where(own == z + 1, state, inflow)
    gain = rows_nt(inflow, unit_ref[0], unit_ref[1])
    solved = s_ref[...] + (gain * half_grow) * top_ref[:, 0:1] * half_grow
    solved = [solved[:, width * k : width * (k + 1)] for k in range(count)]
    state = jnp.zeros((COLS, width), F32)
    running = state
    after = [None] * (count + 1)
    for i in range(max(planes, count) - 1):
        z, j = planes - 1 - i, count - 1 - i
        if z > 0:
            leaving = backs[z]
            if z < planes - 1:
                leaving = leaving + grow * rows_nn(state, pack_ref[z, 0], pack_ref[z, 1])
            state = leaving
            running = jnp.where(own == z - 1, state, running)
        if j > 0:
            right = solved[j] if after[j + 1] is None else solved[j] - after[j + 1]
            after[j] = rows_nn(right, m_ref[j, 0], m_ref[j, 1])
    gain = rows_nn(running, late_ref[0], late_ref[1])
    gain = (gain * half_grow) * late_top_ref[:, 0:1] * half_grow
    answers = []
    for j in range(count):
        if j < count - 1:
            right = solved[j] - (after[j + 1] + gain[:, width * (j + 1) : width * (j + 2)])
        else:
            right = solved[j] - running
        answers.append(rows_nn(right, m_ref[j, 2]))
    coarse = jnp.concatenate(answers, axis=0).astype(BF16)
    for z in range(x_ref.shape[0]):
        x_ref[z] = coarse


def choose_kernel(plane_size, z_ref, c_ref, x_ref, other_ref, code_ref, send_ref):
    peers, tiles, rows, width = send_ref.shape
    planes = x_ref.shape[0]
    body = code_ref.shape[0]
    core = c_ref[0]
    lane = lax.broadcasted_iota(jnp.int32, (body, planes * plane_size * COLS), 1)
    codes = code_ref[...].astype(jnp.int32)
    x_count = plane_size // 2
    mine, theirs = x_ref[...].astype(F32), other_ref[...].astype(F32)
    halves = [jnp.where(core == half, mine, theirs).reshape(lane.shape[1], width) for half in range(2)]
    values = jnp.concatenate(halves, axis=1).astype(BF16)
    mine, theirs = x_ref[z_ref[0]].astype(F32), other_ref[z_ref[0]].astype(F32)
    own = [jnp.where(core == half, mine, theirs) for half in range(2)]
    for d in range(peers):
        pick = (lane == codes[:, d : d + 1]).astype(F32).astype(BF16)
        chosen = jnp.dot(pick, values, preferred_element_type=F32).astype(BF16)
        for half in range(2):
            part = chosen[:, width * half : width * (half + 1)].reshape(body // rows, rows, width)
            for pair in range(body // rows):
                send_ref[d, 2 * pair + half] = part[pair]
        j = 2 * (d % x_count)
        ends = [
            jnp.where(
                core == 0, own[half][COLS * j : COLS * (j + 1)], own[half][COLS * (j + 1) : COLS * (j + 2)]
            )
            for half in range(2)
        ]
        send_ref[d, tiles - 1] = jnp.concatenate(ends, axis=0).astype(BF16)


def leaf_backward_kernel(w_ref, tail_ref, fwd_ref, inv_ref, upd_ref, out_ref, anc_ref):
    step = pl.program_id(0)
    peers, _, rows, width = w_ref.shape
    rhs_count = fwd_ref.shape[1]
    for pair in range(LEAF_STEP // 2):
        came = [w_ref[:, 2 * pair + half].astype(F32) for half in range(2)]
        for k in range(2):
            leaf = 2 * pair + k
            both = jnp.concatenate([c[:, k * COLS : (k + 1) * COLS, :] for c in came], axis=1)
            chosen = both.reshape(rhs_count, width).astype(BF16)
            correction = jnp.dot(chosen, upd_ref[leaf], preferred_element_type=F32)
            residue = (fwd_ref[leaf].astype(F32) - correction).astype(BF16)
            out_ref[leaf] = lax.dot_general(
                inv_ref[leaf], residue, (((0,), (1,)), ((), ())), preferred_element_type=F32
            ).astype(BF16)

    @pl.when(step == 0)
    def _():
        anc_ref[...] = tail_ref[:, 0].astype(F32).reshape(rhs_count, width).T


SMEM = pl.BlockSpec(memory_space=pltpu.SMEM)


def call(kernel, operands, outs, scratch=(), flops=0, after=(), vmem=16):
    moved = sum(a.size * a.dtype.itemsize for a in list(operands) + list(outs))
    if after:
        inner, count = kernel, len(operands)
        kernel = lambda *refs: inner(*refs[:count], *refs[count + len(after) :])
    return pl.pallas_call(
        kernel,
        out_shape=outs,
        in_specs=[
            SMEM if a.dtype == jnp.int32 else pl.BlockSpec(memory_space=pltpu.VMEM) for a in operands
        ]
        + [pl.BlockSpec(memory_space=pl.ANY) for _ in after],
        out_specs=[pl.BlockSpec(memory_space=pltpu.VMEM) for _ in outs],
        scratch_shapes=list(scratch),
        compiler_params=pltpu.CompilerParams(vmem_limit_bytes=vmem * 2**20),
        cost_estimate=pl.CostEstimate(flops=flops, bytes_accessed=moved, transcendentals=0),
    )(*operands, *after)


def shift(value, axis, by):
    size = lax.axis_size(axis)
    return lax.ppermute(value, axis, [((i + by) % size, i) for i in range(size)])


def every_other(value, by):
    half = lax.axis_size("z") // 2
    return lax.ppermute(
        value,
        ("z", "c"),
        [
            (2 * (2 * ((z // 2 + by) % half) + c) + z % 2, 2 * z + c)
            for z in range(2 * half)
            for c in range(2)
        ],
    )


def local(leaf_rhs, leaf_inverse, leaf_update, leaf_target, anc_rhs, anc_inverse, anc_coupling):
    rhs, inv, upd = leaf_rhs[0], leaf_inverse[0], leaf_update[0]
    leaves, width, rhs_count = rhs.shape
    peers = lax.axis_size(PLANE_AXES)
    both_peers = 2 * peers
    planes = lax.axis_size("z")
    x_count = lax.axis_size("x")
    plane_size = 2 * x_count
    chain = planes * plane_size
    pairs = leaves // 2
    sds = jax.ShapeDtypeStruct
    y_index, z_index, x_index, c_index = (
        lax.axis_index(a).astype(jnp.int32).reshape(1) for a in ("y", "z", "x", "c")
    )

    (own_pair,) = call(own_pair_kernel, (anc_inverse, anc_coupling), [sds((3, width, width), BF16)], vmem=60)
    along = [own_pair] + [shift(own_pair, "x", d) for d in range(1, x_count)]

    whole = lambda shape: pl.BlockSpec(shape, lambda i: (0,) * len(shape))
    sent = (both_peers, pairs + 1, 2 * COLS, width)
    forward, send = pl.pallas_call(
        leaf_forward_kernel,
        grid=(1,),
        out_shape=[sds((leaves, rhs_count, width), BF16), sds(sent, BF16)],
        in_specs=[SMEM, SMEM] + [whole(a.shape) for a in (rhs, inv, upd, anc_rhs[0])],
        out_specs=[whole((leaves, rhs_count, width)), whole(sent)],
        compiler_params=pltpu.CompilerParams(
            dimension_semantics=("arbitrary",), vmem_limit_bytes=60 * 2**20
        ),
    )(y_index, leaf_target.astype(jnp.int32).reshape(leaves), rhs, inv, upd, anc_rhs[0])

    send, *along = lax.optimization_barrier((send, *along))
    came = lax.all_to_all(send.reshape(both_peers, -1, width), CORE_AXES, 0, 0, tiled=True).reshape(sent)

    across = [shift(pair, "c", 1) for pair in along]
    m_blocks, pack, unit, top = call(
        functools.partial(transfer_kernel, x_count),
        (x_index, c_index, *along, *across),
        [
            sds((plane_size, 3, width, width), BF16),
            sds((3, width, width), BF16),
            sds((2, plane_size * width, width), BF16),
            sds((COLS, width), F32),
        ],
    )
    steps = sorted(range(planes // 2), key=lambda d: -abs(d - planes // 4))
    packs = [every_other(pack, d) for d in steps]

    dense, codes = call(
        functools.partial(densify_kernel, plane_size),
        (z_index, c_index, came),
        [
            sds((planes, plane_size * COLS, width), BF16),
            sds((leaves * COLS, peers), F32),
        ],
        scratch=[pltpu.VMEM((chain * COLS, width), F32)],
    )
    dense, *packs = lax.optimization_barrier((dense, *packs))
    sums = lax.all_to_all(dense, "z", 0, 0, tiled=True)
    (own_packs,) = call(functools.partial(order_kernel, steps), (z_index, *packs), [sds((planes // 2, 3, width, width), BF16)])
    other_packs = shift(own_packs, "c", 1)
    late, late_top = call(
        late_kernel,
        (m_blocks,),
        [sds((2, width, plane_size * width), BF16), sds((COLS, width), F32)],
    )
    s_wide, ends = call(
        block_solve_kernel,
        (sums, m_blocks, unit, top),
        [sds((COLS, plane_size * width), F32), sds((planes, 3 * COLS, width), F32)],
    )
    ends, other_packs, late, late_top = lax.optimization_barrier((ends, other_packs, late, late_top))
    all_ends = lax.all_to_all(ends, "z", 0, 0, tiled=True)
    (x_rows,) = call(
        carry_kernel,
        (z_index, c_index, all_ends, own_packs, other_packs, s_wide, m_blocks, unit, top, late, late_top),
        [sds((planes, plane_size * COLS, width), BF16)],
        scratch=[pltpu.VMEM((planes, 3, width, width), BF16)],
    )
    all_x = lax.all_to_all(x_rows, "z", 0, 0, tiled=True)
    other_x = shift(all_x, "c", 1)
    (answer,) = call(
        functools.partial(choose_kernel, plane_size),
        (z_index, c_index, all_x, other_x, codes),
        [sds((peers, 2 * pairs + 1, 2 * COLS, width), BF16)],
    )
    answers = lax.all_to_all(answer.reshape(peers, -1, width), PLANE_AXES, 0, 0, tiled=True)
    answers = answers.reshape(answer.shape)

    leaf = lambda i: (i, 0, 0)
    leaf_solution, anc_solution = pl.pallas_call(
        leaf_backward_kernel,
        grid=(leaves // LEAF_STEP,),
        out_shape=[sds((leaves, width, rhs_count), BF16), sds((width, rhs_count), F32)],
        in_specs=[
            pl.BlockSpec((peers, LEAF_STEP, 2 * COLS, width), lambda i: (0, i, 0, 0)),
            pl.BlockSpec((peers, 1, 2 * COLS, width), lambda i: (0, 2 * pairs, 0, 0)),
            pl.BlockSpec((LEAF_STEP, rhs_count, width), leaf),
            pl.BlockSpec((LEAF_STEP, width, width), leaf),
            pl.BlockSpec((LEAF_STEP, width, width), leaf),
        ],
        out_specs=[
            pl.BlockSpec((LEAF_STEP, width, rhs_count), leaf),
            pl.BlockSpec((width, rhs_count), lambda i: (0, 0)),
        ],
        compiler_params=pltpu.CompilerParams(
            dimension_semantics=("arbitrary",), vmem_limit_bytes=40 * 2**20
        ),
    )(answers, answers, forward, inv, upd)
    return (leaf_solution[None], anc_solution[None])


def build(mesh, sizes):
    inner = Mesh(mesh.devices.reshape(sizes), ("y", "z", "x", "c"))
    leaf4 = P("y", ("z", "x", "c"), None, None)
    owner = P(("z", "x", "c"), None, None)
    return jax.shard_map(
        local,
        mesh=inner,
        in_specs=(leaf4, leaf4, leaf4, P("y", ("z", "x", "c"), None), owner, owner, owner),
        out_specs=(leaf4, owner),
        check_vma=False,
    )


def solution(mesh):
    return build(mesh, (4, 8, 4, 2))
```

```python
import functools

import jax
import jax.numpy as jnp
from jax import lax
from jax.experimental import pallas as pl
from jax.experimental.pallas import tpu as pltpu
from jax.sharding import Mesh
from jax.sharding import PartitionSpec as P

F32 = jnp.float32
BF16 = jnp.bfloat16
PLANE_AXES = ("y", "x")
CORE_AXES = ("y", "x", "c")
STEP_SCALE = 2.0**-8
COLS = 8
LEAF_STEP = 16


def dot_nn(a, b):
    return lax.dot_general(
        a, b, (((1,), (0,)), ((), ())), precision=lax.Precision.HIGHEST, preferred_element_type=F32
    )


def split(value):
    high = value.astype(BF16)
    return high, (value - high.astype(F32)).astype(BF16)


def rows_by(rows, parts, contract):
    count = rows.shape[0]
    high, low = split(rows)
    dims = (((1,), (contract,)), ((), ()))
    both = jnp.concatenate([high.astype(F32), low.astype(F32)], axis=0).astype(BF16)
    first = lax.dot_general(both, parts[0], dims, preferred_element_type=F32)
    total = first[:count] + first[count:]
    if len(parts) > 1:
        total = total + lax.dot_general(high, parts[1], dims, preferred_element_type=F32)
    return total


def rows_nn(rows, *parts):
    return rows_by(rows, parts, 0)


def rows_nt(rows, *parts):
    return rows_by(rows, parts, 1)


def leaf_forward_kernel(y_ref, tgt_ref, rhs_ref, inv_ref, upd_ref, anc_ref, fwd_ref, send_ref):
    rhs_count, width = fwd_ref.shape[1:]
    peers, tiles = send_ref.shape[0:2]
    for pair in range(tiles - 1):
        parts = []
        for k in range(2):
            leaf = 2 * pair + k
            forward = lax.dot_general(
                rhs_ref[leaf], inv_ref[leaf], (((0,), (1,)), ((), ())), preferred_element_type=F32
            ).astype(BF16)
            fwd_ref[leaf] = forward
            update = lax.dot_general(
                forward, upd_ref[leaf], (((1,), (1,)), ((), ())), preferred_element_type=F32
            )
            parts.append(update.reshape(peers, COLS, width))
        send_ref[:, pair] = jnp.concatenate(parts, axis=1).astype(BF16)
    rows = anc_ref[...].T
    high = rows.astype(BF16).astype(F32)
    layer = y_ref[0]
    mine = jnp.where(layer == 0, high, jnp.where(layer == 1, rows - high, jnp.zeros_like(rows)))
    leaf = lax.broadcasted_iota(jnp.int32, (COLS, width), 1) // COLS
    names = jnp.zeros((COLS, width), F32)
    for k in range(tgt_ref.shape[0]):
        names = jnp.where(leaf == k, tgt_ref[k].astype(F32), names)
    names = jnp.broadcast_to(names[None], (peers, COLS, width))
    send_ref[:, tiles - 1] = jnp.concatenate([mine.reshape(peers, COLS, width), names], axis=1).astype(BF16)


def own_pair_kernel(inv_ref, cpl_ref, out_ref):
    inverse = inv_ref[0]
    out_ref[0], out_ref[1] = split(rows_nn(inverse, *split(cpl_ref[0])))
    out_ref[2] = inverse.astype(BF16)


def transfer_kernel(x_count, x_ref, c_ref, *refs):
    pairs = refs[: 2 * x_count]
    m_ref, pack_ref, unit_ref, top_ref = refs[-4:]
    count, _, width = m_ref.shape[0:3]
    x, core = x_ref[0], c_ref[0]
    for d in range(x_count):
        for other in range(2):
            place = 2 * lax.rem(x + d, x_count) + jnp.where(other == 0, core, 1 - core)
            m_ref[place] = pairs[other * x_count + d][...]
    half = count // 2
    runs = []
    for k in range(count):
        if k % half == 0:
            run = m_ref[k, 0].astype(F32) + m_ref[k, 1].astype(F32)
        else:
            high, low = split(runs[-1])
            run = jnp.dot(m_ref[k, 0], high, preferred_element_type=F32)
            run += jnp.dot(m_ref[k, 0], low, preferred_element_type=F32)
            run += jnp.dot(m_ref[k, 1], high, preferred_element_type=F32)
        runs.append(run * -STEP_SCALE)
    first = jnp.concatenate(
        [runs[k] * STEP_SCALE ** (count - 1 - k) for k in range(half)], axis=0
    )
    second = jnp.concatenate(
        [runs[k] * STEP_SCALE ** (count - 1 - k) for k in range(half, count)], axis=0
    )
    second = rows_nn(second, *split(runs[half - 1]))
    stack = jnp.concatenate([first, second], axis=0)
    top = jnp.maximum(jnp.max(jnp.abs(stack)), 1e-30)
    unit = stack * (1.0 / top)
    unit_ref[0], unit_ref[1] = split(unit)
    high, low = split(unit.T)
    gram = lax.dot_general(high, high, (((1,), (1,)), ((), ())), preferred_element_type=F32)
    cross = lax.dot_general(high, low, (((1,), (1,)), ((), ())), preferred_element_type=F32)
    pack_ref[0], pack_ref[1] = split(stack[width * (count - 1) :])
    pack_ref[2] = (gram + (cross + cross.T)).astype(BF16)
    top_ref[...] = jnp.full(top_ref.shape, top, F32)


def late_kernel(m_ref, late_ref, top_ref):
    count = m_ref.shape[0]
    half = count // 2
    runs = [None] * count
    for k in reversed(range(count)):
        if k % half == half - 1:
            run = m_ref[k, 0].astype(F32) + m_ref[k, 1].astype(F32)
        else:
            run = rows_nn(runs[k + 1], m_ref[k, 0], m_ref[k, 1])
        runs[k] = run * -STEP_SCALE
    shared = runs[half]
    first = rows_nn(shared, *split(jnp.concatenate(runs[:half], axis=1)))
    width = shared.shape[0]
    pieces = [first[:, width * k : width * (k + 1)] for k in range(half)] + runs[half:]
    stack = jnp.concatenate([pieces[k] * STEP_SCALE**k for k in range(count)], axis=1)
    top = jnp.maximum(jnp.max(jnp.abs(stack)), 1e-30)
    late_ref[0], late_ref[1] = split(stack * (1.0 / top))
    top_ref[...] = jnp.full(top_ref.shape, top, F32)


def order_kernel(steps, z_ref, *refs):
    out_ref = refs[-1]
    count = out_ref.shape[0]
    for i, d in enumerate(steps):
        out_ref[lax.rem(z_ref[0] // 2 + d, count)] = refs[i][...]


def densify_kernel(plane_size, z_ref, c_ref, v_ref, dense_ref, code_ref, acc_ref):
    sources, tiles, rows, width = v_ref.shape
    planes = dense_ref.shape[0]
    body = (tiles - 1) * rows
    lane = lax.broadcasted_iota(jnp.int32, (sources, body), 1)
    last = v_ref[:, tiles - 1].astype(F32)
    codes = last[:, COLS, :].astype(jnp.int32) * COLS + lane % COLS
    by_core = codes.astype(F32).reshape(sources // 2, 2, body)
    code_ref[...] = jnp.where(c_ref[0] == 0, by_core[:, 0], by_core[:, 1]).T
    row = lax.broadcasted_iota(jnp.int32, (acc_ref.shape[0], body), 0)
    total = None
    for s in range(0, sources, 2):
        pick = jnp.concatenate(
            [(row == codes[s + i : s + i + 1, :]).astype(F32).astype(BF16) for i in range(2)], axis=1
        )
        both = v_ref[s : s + 2, 0 : tiles - 1].reshape(2 * body, width)
        term = jnp.dot(pick, both, preferred_element_type=F32)
        total = term if total is None else total + term
    acc_ref[...] = -total
    own = pl.multiple_of(z_ref[0] * plane_size * COLS, plane_size * COLS)
    mine = last[0:plane_size, 0:COLS]
    for y in range(1, sources // plane_size):
        mine = mine + last[y * plane_size : (y + 1) * plane_size, 0:COLS]
    acc_ref[pl.ds(own, plane_size * COLS), :] += mine.reshape(plane_size * COLS, width)
    dense_ref[...] = acc_ref[...].astype(BF16).reshape(dense_ref.shape)


def block_solve_kernel(e_ref, m_ref, unit_ref, top_ref, s_ref, out_ref):
    count = m_ref.shape[0]
    reduced = e_ref[0].astype(F32)
    for s in range(1, e_ref.shape[0]):
        reduced = reduced + e_ref[s].astype(F32)
    solved = []
    for j in range(count):
        b = rows_nt(reduced[COLS * j : COLS * (j + 1)], m_ref[j, 2])
        if j > 0:
            b = b - rows_nt(solved[-1], m_ref[j, 0], m_ref[j, 1])
        solved.append(b)
    half_grow = STEP_SCALE ** (-count // 2)
    solved_wide = jnp.concatenate(solved, axis=1)
    s_ref[...] = solved_wide
    back = rows_nn(solved_wide, unit_ref[0], unit_ref[1])
    back = -((back * half_grow) * top_ref[...] * half_grow)
    ends = jnp.concatenate([solved[-1], back, top_ref[...]], axis=0)
    for z in range(out_ref.shape[0]):
        out_ref[z] = ends


def carry_kernel(
    z_ref, c_ref, ends_ref, mine_ref, other_ref, s_ref, m_ref, unit_ref, top_ref, late_ref, late_top_ref, x_ref, pack_ref
):
    planes = ends_ref.shape[0]
    count, _, width = m_ref.shape[0:3]
    core = c_ref[0]
    for i in range(planes // 2):
        pack_ref[2 * i + core] = mine_ref[i]
        pack_ref[2 * i + 1 - core] = other_ref[i]
    grow = STEP_SCALE**-count
    half_grow = STEP_SCALE ** (-count // 2)
    own = z_ref[0]
    state = jnp.zeros((COLS, width), F32)
    inflow = state
    backs = []
    for z in range(planes):
        leaving, back, top = (ends_ref[z, COLS * i : COLS * (i + 1)] for i in range(3))
        if z > 0:
            answer = rows_nn(state, pack_ref[z, 2])
            for _ in range(2):
                answer = (answer * half_grow) * top * half_grow
            back = back - answer
            leaving = leaving + grow * rows_nt(state, pack_ref[z, 0], pack_ref[z, 1])
        backs.append(back)
        state = leaving
        if z < planes - 1:
            inflow = jnp.where(own == z + 1, state, inflow)
    gain = rows_nt(inflow, unit_ref[0], unit_ref[1])
    solved = s_ref[...] + (gain * half_grow) * top_ref[:, 0:1] * half_grow
    solved = [solved[:, width * k : width * (k + 1)] for k in range(count)]
    state = jnp.zeros((COLS, width), F32)
    running = state
    after = [None] * (count + 1)
    for i in range(max(planes, count) - 1):
        z, j = planes - 1 - i, count - 1 - i
        if z > 0:
            leaving = backs[z]
            if z < planes - 1:
                leaving = leaving + grow * rows_nn(state, pack_ref[z, 0], pack_ref[z, 1])
            state = leaving
            running = jnp.where(own == z - 1, state, running)
        if j > 0:
            right = solved[j] if after[j + 1] is None else solved[j] - after[j + 1]
            after[j] = rows_nn(right, m_ref[j, 0], m_ref[j, 1])
    gain = rows_nn(running, late_ref[0], late_ref[1])
    gain = (gain * half_grow) * late_top_ref[:, 0:1] * half_grow
    answers = []
    for j in range(count):
        if j < count - 1:
            right = solved[j] - (after[j + 1] + gain[:, width * (j + 1) : width * (j + 2)])
        else:
            right = solved[j] - running
        answers.append(rows_nn(right, m_ref[j, 2]))
    coarse = jnp.concatenate(answers, axis=0).astype(BF16)
    for z in range(x_ref.shape[0]):
        x_ref[z] = coarse


def choose_kernel(plane_size, z_ref, c_ref, x_ref, other_ref, code_ref, send_ref):
    peers, tiles, rows, width = send_ref.shape
    planes = x_ref.shape[0]
    body = code_ref.shape[0]
    core = c_ref[0]
    lane = lax.broadcasted_iota(jnp.int32, (body, planes * plane_size * COLS), 1)
    codes = code_ref[...].astype(jnp.int32)
    x_count = plane_size // 2
    mine, theirs = x_ref[...].astype(F32), other_ref[...].astype(F32)
    halves = [jnp.where(core == half, mine, theirs).reshape(lane.shape[1], width) for half in range(2)]
    values = jnp.concatenate(halves, axis=1).astype(BF16)
    mine, theirs = x_ref[z_ref[0]].astype(F32), other_ref[z_ref[0]].astype(F32)
    own = [jnp.where(core == half, mine, theirs) for half in range(2)]
    for d in range(peers):
        pick = (lane == codes[:, d : d + 1]).astype(F32).astype(BF16)
        chosen = jnp.dot(pick, values, preferred_element_type=F32).astype(BF16)
        for half in range(2):
            part = chosen[:, width * half : width * (half + 1)].reshape(body // rows, rows, width)
            for pair in range(body // rows):
                send_ref[d, 2 * pair + half] = part[pair]
        j = 2 * (d % x_count)
        ends = [
            jnp.where(
                core == 0, own[half][COLS * j : COLS * (j + 1)], own[half][COLS * (j + 1) : COLS * (j + 2)]
            )
            for half in range(2)
        ]
        send_ref[d, tiles - 1] = jnp.concatenate(ends, axis=0).astype(BF16)


def leaf_backward_kernel(w_ref, tail_ref, fwd_ref, inv_ref, upd_ref, out_ref, anc_ref):
    step = pl.program_id(0)
    peers, _, rows, width = w_ref.shape
    rhs_count = fwd_ref.shape[1]
    for pair in range(LEAF_STEP // 2):
        came = [w_ref[:, 2 * pair + half].astype(F32) for half in range(2)]
        for k in range(2):
            leaf = 2 * pair + k
            both = jnp.concatenate([c[:, k * COLS : (k + 1) * COLS, :] for c in came], axis=1)
            chosen = both.reshape(rhs_count, width).astype(BF16)
            correction = jnp.dot(chosen, upd_ref[leaf], preferred_element_type=F32)
            residue = (fwd_ref[leaf].astype(F32) - correction).astype(BF16)
            out_ref[leaf] = lax.dot_general(
                inv_ref[leaf], residue, (((0,), (1,)), ((), ())), preferred_element_type=F32
            ).astype(BF16)

    @pl.when(step == 0)
    def _():
        anc_ref[...] = tail_ref[:, 0].astype(F32).reshape(rhs_count, width).T


SMEM = pl.BlockSpec(memory_space=pltpu.SMEM)


def call(kernel, operands, outs, scratch=(), flops=0, after=(), vmem=16):
    moved = sum(a.size * a.dtype.itemsize for a in list(operands) + list(outs))
    if after:
        inner, count = kernel, len(operands)
        kernel = lambda *refs: inner(*refs[:count], *refs[count + len(after) :])
    return pl.pallas_call(
        kernel,
        out_shape=outs,
        in_specs=[
            SMEM if a.dtype == jnp.int32 else pl.BlockSpec(memory_space=pltpu.VMEM) for a in operands
        ]
        + [pl.BlockSpec(memory_space=pl.ANY) for _ in after],
        out_specs=[pl.BlockSpec(memory_space=pltpu.VMEM) for _ in outs],
        scratch_shapes=list(scratch),
        compiler_params=pltpu.CompilerParams(vmem_limit_bytes=vmem * 2**20),
        cost_estimate=pl.CostEstimate(flops=flops, bytes_accessed=moved, transcendentals=0),
    )(*operands, *after)


def shift(value, axis, by):
    size = lax.axis_size(axis)
    return lax.ppermute(value, axis, [((i + by) % size, i) for i in range(size)])


def every_other(value, by):
    half = lax.axis_size("z") // 2
    return lax.ppermute(
        value,
        ("z", "c"),
        [
            (2 * (2 * ((z // 2 + by) % half) + c) + z % 2, 2 * z + c)
            for z in range(2 * half)
            for c in range(2)
        ],
    )


def local(leaf_rhs, leaf_inverse, leaf_update, leaf_target, anc_rhs, anc_inverse, anc_coupling):
    rhs, inv, upd = leaf_rhs[0], leaf_inverse[0], leaf_update[0]
    leaves, width, rhs_count = rhs.shape
    peers = lax.axis_size(PLANE_AXES)
    both_peers = 2 * peers
    planes = lax.axis_size("z")
    x_count = lax.axis_size("x")
    plane_size = 2 * x_count
    chain = planes * plane_size
    pairs = leaves // 2
    sds = jax.ShapeDtypeStruct
    y_index, z_index, x_index, c_index = (
        lax.axis_index(a).astype(jnp.int32).reshape(1) for a in ("y", "z", "x", "c")
    )

    (own_pair,) = call(own_pair_kernel, (anc_inverse, anc_coupling), [sds((3, width, width), BF16)], vmem=60)
    along = [own_pair] + [shift(own_pair, "x", d) for d in range(1, x_count)]

    whole = lambda shape: pl.BlockSpec(shape, lambda i: (0,) * len(shape))
    sent = (both_peers, pairs + 1, 2 * COLS, width)
    forward, send = pl.pallas_call(
        leaf_forward_kernel,
        grid=(1,),
        out_shape=[sds((leaves, rhs_count, width), BF16), sds(sent, BF16)],
        in_specs=[SMEM, SMEM] + [whole(a.shape) for a in (rhs, inv, upd, anc_rhs[0])],
        out_specs=[whole((leaves, rhs_count, width)), whole(sent)],
        compiler_params=pltpu.CompilerParams(
            dimension_semantics=("arbitrary",), vmem_limit_bytes=60 * 2**20
        ),
    )(y_index, leaf_target.astype(jnp.int32).reshape(leaves), rhs, inv, upd, anc_rhs[0])

    send, *along = lax.optimization_barrier((send, *along))
    came = lax.all_to_all(send.reshape(both_peers, -1, width), CORE_AXES, 0, 0, tiled=True).reshape(sent)

    across = [shift(pair, "c", 1) for pair in along]
    m_blocks, pack, unit, top = call(
        functools.partial(transfer_kernel, x_count),
        (x_index, c_index, *along, *across),
        [
            sds((plane_size, 3, width, width), BF16),
            sds((3, width, width), BF16),
            sds((2, plane_size * width, width), BF16),
            sds((COLS, width), F32),
        ],
    )
    steps = sorted(range(planes // 2), key=lambda d: -abs(d - planes // 4))
    packs = [every_other(pack, d) for d in steps]

    dense, codes = call(
        functools.partial(densify_kernel, plane_size),
        (z_index, c_index, came),
        [
            sds((planes, plane_size * COLS, width), BF16),
            sds((leaves * COLS, peers), F32),
        ],
        scratch=[pltpu.VMEM((chain * COLS, width), F32)],
    )
    dense, *packs = lax.optimization_barrier((dense, *packs))
    sums = lax.all_to_all(dense, "z", 0, 0, tiled=True)
    (own_packs,) = call(functools.partial(order_kernel, steps), (z_index, *packs), [sds((planes // 2, 3, width, width), BF16)])
    other_packs = shift(own_packs, "c", 1)
    late, late_top = call(
        late_kernel,
        (m_blocks,),
        [sds((2, width, plane_size * width), BF16), sds((COLS, width), F32)],
    )
    s_wide, ends = call(
        block_solve_kernel,
        (sums, m_blocks, unit, top),
        [sds((COLS, plane_size * width), F32), sds((planes, 3 * COLS, width), F32)],
    )
    ends, other_packs, late, late_top = lax.optimization_barrier((ends, other_packs, late, late_top))
    all_ends = lax.all_to_all(ends, "z", 0, 0, tiled=True)
    (x_rows,) = call(
        carry_kernel,
        (z_index, c_index, all_ends, own_packs, other_packs, s_wide, m_blocks, unit, top, late, late_top),
        [sds((planes, plane_size * COLS, width), BF16)],
        scratch=[pltpu.VMEM((planes, 3, width, width), BF16)],
    )
    all_x = lax.all_to_all(x_rows, "z", 0, 0, tiled=True)
    other_x = shift(all_x, "c", 1)
    (answer,) = call(
        functools.partial(choose_kernel, plane_size),
        (z_index, c_index, all_x, other_x, codes),
        [sds((peers, 2 * pairs + 1, 2 * COLS, width), BF16)],
    )
    answers = lax.all_to_all(answer.reshape(peers, -1, width), PLANE_AXES, 0, 0, tiled=True)
    answers = answers.reshape(answer.shape)

    leaf = lambda i: (i, 0, 0)
    leaf_solution, anc_solution = pl.pallas_call(
        leaf_backward_kernel,
        grid=(leaves // LEAF_STEP,),
        out_shape=[sds((leaves, width, rhs_count), BF16), sds((width, rhs_count), F32)],
        in_specs=[
            pl.BlockSpec((peers, LEAF_STEP, 2 * COLS, width), lambda i: (0, i, 0, 0)),
            pl.BlockSpec((peers, 1, 2 * COLS, width), lambda i: (0, 2 * pairs, 0, 0)),
            pl.BlockSpec((LEAF_STEP, rhs_count, width), leaf),
            pl.BlockSpec((LEAF_STEP, width, width), leaf),
            pl.BlockSpec((LEAF_STEP, width, width), leaf),
        ],
        out_specs=[
            pl.BlockSpec((LEAF_STEP, width, rhs_count), leaf),
            pl.BlockSpec((width, rhs_count), lambda i: (0, 0)),
        ],
        compiler_params=pltpu.CompilerParams(
            dimension_semantics=("arbitrary",), vmem_limit_bytes=40 * 2**20
        ),
    )(answers, answers, forward, inv, upd)
    return (leaf_solution[None], anc_solution[None])


def build(mesh, sizes):
    inner = Mesh(mesh.devices.reshape(sizes), ("y", "z", "x", "c"))
    leaf4 = P("y", ("z", "x", "c"), None, None)
    owner = P(("z", "x", "c"), None, None)
    return jax.shard_map(
        local,
        mesh=inner,
        in_specs=(leaf4, leaf4, leaf4, P("y", ("z", "x", "c"), None), owner, owner, owner),
        out_specs=(leaf4, owner),
        check_vma=False,
    )


def solution(mesh):
    return build(mesh, (4, 8, 4, 2))
```
